128 devices in a mesh: box: 8 (over y, core), dir: 16 (over x, z).
Axes of the slice: x: 4, y: 4, z: 4, core: 2. Of those that a mesh axis runs over, the one named last changes fastest.
Arguments:
- currents: bfloat16 [1024, 2, 256, 128], P(('box', 'dir')), may hold values from -6 to 6
- near_blocks: bfloat16 [1024, 3, 2, 256, 256], P(('box', 'dir')), may hold values from -0.21875 to 0.21875
- near_mask: int32 [2, 1024], replicated, may hold values 0 or 1
- aggregate: bfloat16 [2, 512, 256], replicated, may hold values from -0.375 to 0.375
- disaggregate: bfloat16 [2, 256, 512], replicated, may hold values from -0.25 to 0.25
- centers: float32 [3, 1024], replicated, may hold values from 0 to 16
Outputs:
- fields: bfloat16 [1024, 2, 256, 128], P(('box', 'dir'))
The draws below stay inside these ranges and needn't reach their ends.
All inputs are finite; a program needn't handle non-finite values.
Results may differ from the reference program's by a relative error of at most 0.0054.
Values may be sent and summed in bfloat16 or wider, within the bound.
A program may use at most 64 MiB of HBM per device.

```python
import math
import jax
import jax.numpy as jnp
from jax import lax

NU = 256
K = 512
A = 128
BOXES = 1024


def plant(values, rng, smallest, largest):
    extent = values.shape
    spot = [jax.random.randint(jax.random.fold_in(rng, axis), (), 0, extent[axis]) for axis in range(len(extent))]
    values = values.at[tuple(spot)].set(smallest)
    longest = extent.index(max(extent))
    spot[longest] = (spot[longest] + 1) % extent[longest]
    return values.at[tuple(spot)].set(largest)


def shard_levels(key, shape, split, least, largest):
    def one(position, shards_of):
        draws = jax.random.uniform(jax.random.fold_in(jax.random.fold_in(key, 6), position), (shards_of,), jnp.float32, least / len(split), largest / len(split))
        return jnp.repeat(jnp.exp(draws), shape[position] // shards_of).reshape((-1,) + (1,) * (len(shape) - position - 1))

    factor_of = one(*split[0])
    for cut in split[1:]:
        factor_of = factor_of * one(*cut)
    return factor_of


def centred(own_key, dims, scale, limit, pieces=(), held_as=jnp.bfloat16):
    entries = jax.random.normal(own_key, dims, jnp.float32) * scale
    if len(pieces) > 0:
        entries = shard_levels(own_key, dims, pieces, -0.22, 0.18) * entries
    return jnp.clip(entries, min=-limit, max=limit).astype(held_as)


def setup_inputs(seed: int = 0) -> dict:
    key_list = jax.random.split(jax.random.key(seed), 7)
    currents = centred(key_list[0], (BOXES, 2, NU, A), 1.0, 6.0, ((0, 128),))
    near_blocks = centred(key_list[1], (BOXES, 3, 2, NU, NU), (3 * NU) ** -0.5, 0.21875, ((0, 128),))
    near_mask = plant((jax.random.randint(key_list[2], (2, BOXES), 0, 4) < 3).astype(jnp.int32), jax.random.fold_in(key_list[2], 1), 0, 1)
    aggregate = centred(key_list[3], (2, K, NU), NU ** -0.5, 0.375)
    disaggregate = centred(key_list[4], (2, NU, K), K ** -0.5, 0.25)
    centers = jnp.clip(jax.random.uniform(key_list[5], (3, BOXES), jnp.float32, 0.0, 16.0), 0.0, 16.0)
    return {"currents": currents, "near_blocks": near_blocks, "near_mask": near_mask, "aggregate": aggregate, "disaggregate": disaggregate, "centers": centers}


wave_number = 2.0
far_gain = 8.0
golden_turn = 2.399963229728653

def direction_cosines(count, first, many):
    order = (first + jnp.arange(many, dtype=jnp.int32)).astype(jnp.float32)
    height = 1.0 - (2.0 * order + 1.0) / count
    radial = jnp.sqrt(1.0 - height * height)
    azimuth = order * golden_turn
    return (radial * jnp.cos(azimuth), radial * jnp.sin(azimuth), height)

def phase_angles(points, first, many, count):
    dir_x, dir_y, dir_z = direction_cosines(count, first, many)
    return wave_number * (points[0][:, None] * dir_x[None, :] + points[1][:, None] * dir_y[None, :] + points[2][:, None] * dir_z[None, :])

def far_matrix(centers, near_mask):
    total_boxes = centers.shape[1]
    squared = jnp.zeros((total_boxes, total_boxes), jnp.float32)
    for axis_number in range(3):
        spread = centers[axis_number][:, None] - centers[axis_number][None, :]
        squared = squared + spread * spread
    spacing = jnp.sqrt(1.0 + squared)
    kernel = jnp.cos(wave_number * spacing) / (1.0 + spacing) * (far_gain / math.sqrt(total_boxes))
    rows = jnp.arange(total_boxes, dtype=jnp.int32)[:, None]
    cols = jnp.arange(total_boxes, dtype=jnp.int32)[None, :]
    linked = (cols == rows) | (cols == rows - 1) & (near_mask[0][:, None] == 1) | (cols == rows + 1) & (near_mask[1][:, None] == 1)
    return jnp.where(linked, 0.0, kernel).astype(jnp.bfloat16)

def reference(currents, near_blocks, near_mask, aggregate, disaggregate, centers):
    flt = jnp.float32
    total_boxes = centers.shape[1]
    padded = jnp.pad(currents.astype(flt), ((1, 1), (0, 0), (0, 0), (0, 0)))
    left_mask = near_mask[0].astype(flt)
    right_mask = near_mask[1].astype(flt)
    block = math.gcd(total_boxes, 64)

    def near_part(number):
        first_box = number * block
        blocks = lax.dynamic_slice_in_dim(near_blocks, first_box, block, 0).astype(flt)
        window = lax.dynamic_slice_in_dim(padded, first_box, block + 2, 0)
        left_on = lax.dynamic_slice_in_dim(left_mask, first_box, block, 0)[:, None, None, None]
        right_on = lax.dynamic_slice_in_dim(right_mask, first_box, block, 0)[:, None, None, None]
        stacked = jnp.stack([window[1:-1], window[:-2] * left_on, window[2:] * right_on], 1)

        def product(left, right):
            return jnp.einsum('bjuv,bjva->bua', left, right, precision=lax.Precision.HIGHEST)
        near_re = product(blocks[:, :, 0], stacked[:, :, 0]) - product(blocks[:, :, 1], stacked[:, :, 1])
        near_im = product(blocks[:, :, 0], stacked[:, :, 1]) + product(blocks[:, :, 1], stacked[:, :, 0])
        return jnp.stack([near_re, near_im], 1)
    near = lax.map(near_part, jnp.arange(total_boxes // block, dtype=jnp.int32)).reshape(currents.shape)
    translate = far_matrix(centers, near_mask).astype(flt)
    cur_re = currents[:, 0].astype(flt)
    cur_im = currents[:, 1].astype(flt)
    width = math.gcd(K, 32)

    def far_step(carry, number):
        first_dir = number * width
        agg_part = lax.dynamic_slice_in_dim(aggregate, first_dir, width, 1).astype(flt)
        dis_part = lax.dynamic_slice_in_dim(disaggregate, first_dir, width, 2).astype(flt)

        def gather_in(matrix, vectors):
            return jnp.einsum('ku,bua->bka', matrix, vectors, precision=lax.Precision.HIGHEST)
        pat_re = gather_in(agg_part[0], cur_re) - gather_in(agg_part[1], cur_im)
        pat_im = gather_in(agg_part[0], cur_im) + gather_in(agg_part[1], cur_re)
        theta = phase_angles(centers, first_dir, width, K)
        cosine = jnp.cos(theta)[:, :, None]
        sine = jnp.sin(theta)[:, :, None]
        pattern = jnp.stack([cosine * pat_re + sine * pat_im, cosine * pat_im - sine * pat_re], 2).astype(jnp.bfloat16).astype(flt)
        summed = jnp.dot(translate, pattern.reshape(total_boxes, -1), precision=lax.Precision.HIGHEST).reshape(pattern.shape)
        sum_re = summed[:, :, 0]
        sum_im = summed[:, :, 1]
        received = jnp.stack([cosine * sum_re - sine * sum_im, cosine * sum_im + sine * sum_re], 2).astype(jnp.bfloat16).astype(flt)

        def spread_out(matrix, vectors):
            return jnp.einsum('uk,bka->bua', matrix, vectors, precision=lax.Precision.HIGHEST)
        far_re = spread_out(dis_part[0], received[:, :, 0]) - spread_out(dis_part[1], received[:, :, 1])
        far_im = spread_out(dis_part[0], received[:, :, 1]) + spread_out(dis_part[1], received[:, :, 0])
        return (carry + jnp.stack([far_re, far_im], 1), None)
    far, unused = lax.scan(far_step, jnp.zeros(currents.shape, flt), jnp.arange(K // width, dtype=jnp.int32))
    return (near + far).astype(jnp.bfloat16)
```

```python
import functools
import math

import jax
import jax.numpy as jnp
import numpy as np
from jax import lax
from jax.experimental import pallas as pl
from jax.experimental.pallas import tpu as pltpu
from jax.sharding import PartitionSpec as P

MESH = pl.DeviceIdType.MESH
golden_turn = 2.399963229728653
far_gain = 8.0

COS_TERMS = (
    1.0,
    -19.73920440673828,
    64.93911743164062,
    -85.45014190673828,
    60.16762924194336,
    -25.967599868774414,
    6.528658390045166,
)
SIN_TERMS = (
    6.2831854820251465,
    -41.34170150756836,
    81.60513305664062,
    -76.70301818847656,
    42.02592849731445,
    -14.899847030639648,
    3.2381374835968018,
)


def polynomial(terms, x):
    total = x * terms[-1] + terms[-2]
    for term in terms[-3::-1]:
        total = total * x + term
    return total


def direction_turns(count):
    order = np.arange(count, dtype=np.float32)
    height = np.float32(1.0) - (np.float32(2.0) * order + np.float32(1.0)) / np.float32(count)
    radial = np.sqrt(np.float32(1.0) - height * height)
    azimuth = (order * np.float32(golden_turn)).astype(np.float64)
    rows = [radial * np.cos(azimuth), radial * np.sin(azimuth), height.astype(np.float64)]
    table = np.zeros((8, count), np.float32)
    for row, values in enumerate(rows):
        table[row] = (values / math.pi).astype(np.float32)
    return table


def dot_nt(left, right):
    return lax.dot_general(left, right, (((1,), (1,)), ((), ())), preferred_element_type=jnp.float32)


def dot_nn(left, right):
    return jnp.dot(left, right, preferred_element_type=jnp.float32)


def kernel(
    n,
    dirs,
    cur_ref,
    near_hbm,
    mask_ref,
    mask_smem,
    agg_ref,
    dis_ref,
    cen_ref,
    turn_ref,
    out_ref,
    near_v,
    near_sem,
    halo,
    halo_send,
    halo_recv,
    turned,
    out1,
    in1,
    send1,
    recv1,
    columns,
    cos_t,
    sin_t,
    trans,
    pattern,
    out2,
    in2,
    send2,
    recv2,
    padded,
    near_sum,
):
    f32, bf16 = jnp.float32, jnp.bfloat16
    boxes, _, nu, angles = cur_ref.shape
    rows = 2 * boxes
    total = n * boxes
    dir_count = agg_ref.shape[0] // 2
    groups = n // 16
    me = lax.axis_index("box") * dirs + lax.axis_index("dir")

    def place(device):
        return (device // dirs, lax.rem(device, dirs))

    fetch_near = pltpu.make_async_copy(near_hbm, near_v, near_sem)
    fetch_near.start()

    barrier = pltpu.get_barrier_semaphore()

    def greet(step, carry):
        pl.semaphore_signal(
            barrier, inc=1, device_id=place(lax.rem(me + step, n)), device_id_type=MESH
        )
        return carry

    lax.fori_loop(1, n, greet, 0)

    def equal(shape, row_of, col_of):
        row = lax.broadcasted_iota(jnp.int32, shape, 0)
        col = lax.broadcasted_iota(jnp.int32, shape, 1)
        return jnp.where(row_of(row) == col_of(col), 1.0, 0.0).astype(bf16)

    eye_angle = equal((angles, angles), lambda r: r, lambda c: c)
    eye_unknown = equal((nu, nu), lambda r: r, lambda c: c)
    swap = equal((256, 256), lambda r: r, lambda c: (c & 15) * 16 + (c >> 4))

    def turn(r, carry):
        block = cur_ref[r & (boxes - 1), r // boxes]
        turned[r] = dot_nt(eye_angle, block).astype(bf16)
        return carry

    lax.fori_loop(0, rows, turn, 0)

    def pack(g, carry):
        first = pl.multiple_of(g * 16, 16)
        block = turned[:, pl.ds(first, 16), :].reshape(256, nu)
        out1[pl.ds(pl.multiple_of(g * 256, 256), 256), :] = dot_nn(swap, block).astype(bf16)
        return carry

    lax.fori_loop(0, groups, pack, 0)

    pl.semaphore_wait(barrier, n - 1)

    def slot(device):
        return pl.ds(pl.multiple_of(device * 16, 16), 16)

    def send_out1(step, carry):
        device = lax.rem(me + step, n)
        pltpu.make_async_remote_copy(
            src_ref=out1.at[slot(device)],
            dst_ref=in1.at[slot(me)],
            send_sem=send1,
            recv_sem=recv1.at[me // 16],
            device_id=place(device),
            device_id_type=MESH,
        ).start()
        return carry

    lax.fori_loop(1, n, send_out1, 0)
    pltpu.make_async_copy(out1.at[slot(me)], in1.at[slot(me)], recv1.at[me // 16]).start()

    to_right = pltpu.make_async_remote_copy(
        src_ref=cur_ref.at[boxes - 1],
        dst_ref=halo.at[0],
        send_sem=halo_send.at[0],
        recv_sem=halo_recv.at[0],
        device_id=place(lax.rem(me + 1, n)),
        device_id_type=MESH,
    )
    to_left = pltpu.make_async_remote_copy(
        src_ref=cur_ref.at[0],
        dst_ref=halo.at[1],
        send_sem=halo_send.at[1],
        recv_sem=halo_recv.at[1],
        device_id=place(lax.rem(me + n - 1, n)),
        device_id_type=MESH,
    )
    to_right.start()
    to_left.start()

    low_row = 0.0 - mask_ref[0:1, :].astype(f32)
    high_row = mask_ref[1:2, :].astype(f32)
    table = jnp.concatenate(
        [cen_ref[...], low_row, high_row, jnp.zeros((3, total), f32)], axis=0
    )
    columns[...] = jnp.transpose(table)

    def phase(step, carry):
        own = pl.ds(pl.multiple_of(step * 8, 8), 8)
        block = columns[own, :]
        turns = (
            block[:, 0:1] * turn_ref[0:1, :]
            + block[:, 1:2] * turn_ref[1:2, :]
            + block[:, 2:3] * turn_ref[2:3, :]
        )
        rest = turns - jnp.round(turns)
        square = rest * rest
        cos_t[own, :] = polynomial(COS_TERMS, square)
        sin_t[own, :] = rest * polynomial(SIN_TERMS, square)
        return carry

    lax.fori_loop(0, total // 8, phase, 0)

    scale = far_gain / math.sqrt(total)

    def translation(step, carry):
        first = pl.multiple_of(step * 16, 16)
        block = columns[pl.ds(first, 16), :]
        row = (lax.broadcasted_iota(jnp.int32, (16, 1), 0) + first).astype(f32)
        low = row + block[:, 3:4]
        high = row + block[:, 4:5]
        for part in range(2):
            wide = slice(part * (total // 2), (part + 1) * (total // 2))
            squared = jnp.ones((16, total // 2), f32)
            for axis in range(3):
                spread = block[:, axis : axis + 1] - cen_ref[axis : axis + 1, wide]
                squared = squared + spread * spread
            spacing = squared * lax.rsqrt(squared)
            turns = spacing * (1.0 / math.pi)
            rest = turns - jnp.round(turns)
            value = polynomial(tuple(scale * t for t in COS_TERMS), rest * rest) / (1.0 + spacing)
            col = (
                lax.broadcasted_iota(jnp.int32, (1, total // 2), 1) + part * (total // 2)
            ).astype(f32)
            linked = (col >= low) & (col <= high)
            trans[pl.ds(first, 16), wide] = jnp.where(linked, 0.0, value).astype(bf16)
        return carry

    lax.fori_loop(0, total // 16, translation, 0)

    def gather(step, carry):
        g = lax.rem(me // 16 + groups - 1 - step, groups)
        span = pl.ds(pl.multiple_of(g * 256, 256), 256)
        pltpu.make_async_copy(in1.at[span], in1.at[span], recv1.at[g]).wait()
        product = dot_nt(in1[span, :], agg_ref[...]).reshape(16, 2, 8, 2 * dir_count)
        real = product[:, 0].reshape(128, 2 * dir_count)
        imag = product[:, 1].reshape(128, 2 * dir_count)
        pat_re = real[:, :dir_count] - imag[:, dir_count:]
        pat_im = real[:, dir_count:] + imag[:, :dir_count]
        own = pl.ds(pl.multiple_of(g * 128, 128), 128)
        cosine = cos_t[own, :]
        sine = sin_t[own, :]
        pattern[own, :dir_count] = (cosine * pat_re + sine * pat_im).astype(bf16)
        pattern[own, dir_count:] = (cosine * pat_im - sine * pat_re).astype(bf16)
        return carry

    lax.fori_loop(0, groups, gather, 0)

    def spread(step, carry):
        q = lax.rem(me // 32 + step, n // 32)
        own = pl.ds(pl.multiple_of(q * 256, 256), 256)
        summed = dot_nn(trans[own, :], pattern[...])
        sum_re = summed[:, :dir_count]
        sum_im = summed[:, dir_count:]
        cosine = cos_t[own, :]
        sine = sin_t[own, :]
        rec_re = (cosine * sum_re - sine * sum_im).astype(bf16)
        rec_im = (cosine * sum_im + sine * sum_re).astype(bf16)
        from_re = dot_nt(rec_re, dis_ref[...])
        from_im = dot_nt(rec_im, dis_ref[...])
        far_re = from_re[:, :nu] - from_im[:, nu:]
        far_im = from_im[:, :nu] + from_re[:, nu:]
        both = jnp.concatenate(
            [far_re.reshape(32, 1, 8, nu), far_im.reshape(32, 1, 8, nu)], axis=1
        ).reshape(512, nu)
        out2[pl.ds(pl.multiple_of(q * 512, 512), 512), :] = both.astype(bf16)

        def send_out2(k, inner):
            device = q * 32 + lax.rem(me + k, 32)

            @pl.when(device != me)
            def _():
                pltpu.make_async_remote_copy(
                    src_ref=out2.at[slot(device)],
                    dst_ref=in2.at[slot(me)],
                    send_sem=send2,
                    recv_sem=recv2.at[me // 16],
                    device_id=place(device),
                    device_id_type=MESH,
                ).start()

            return inner

        lax.fori_loop(0, 32, send_out2, 0)
        return carry

    lax.fori_loop(0, n // 32, spread, 0)
    pltpu.make_async_copy(out2.at[slot(me)], in2.at[slot(me)], recv2.at[me // 16]).start()

    to_right.wait_recv()
    to_left.wait_recv()
    padded[0, :, :angles] = halo[0, 0]
    padded[0, :, angles:] = halo[0, 1]
    padded[boxes + 1, :, :angles] = halo[1, 0]
    padded[boxes + 1, :, angles:] = halo[1, 1]

    def widen(b, carry):
        padded[b + 1, :, :angles] = cur_ref[b, 0]
        padded[b + 1, :, angles:] = cur_ref[b, 1]
        return carry

    lax.fori_loop(0, boxes, widen, 0)
    fetch_near.wait()

    def near(b, carry):
        box = me * boxes + b
        left = jnp.where(box > 0, mask_smem[0, box], 0).astype(f32)
        right = jnp.where(box < total - 1, mask_smem[1, box], 0).astype(f32)
        sides = []
        for part in range(2):
            sides.append(
                dot_nn(near_v[b, 0, part], padded[b + 1])
                + left * dot_nn(near_v[b, 1, part], padded[b])
                + right * dot_nn(near_v[b, 2, part], padded[b + 2])
            )
        near_sum[b, 0] = sides[0][:, :angles] - sides[1][:, angles:]
        near_sum[b, 1] = sides[0][:, angles:] + sides[1][:, :angles]
        return carry

    lax.fori_loop(0, boxes, near, 0)

    def unpack(step, carry):
        g = lax.rem(me // 16 + groups - 1 - step, groups)
        span = pl.ds(pl.multiple_of(g * 256, 256), 256)
        pltpu.make_async_copy(in2.at[span], in2.at[span], recv2.at[g]).wait()
        block = dot_nn(swap, in2[span, :]).astype(bf16).reshape(rows, 16, nu)
        turned[:, pl.ds(pl.multiple_of(g * 16, 16), 16), :] = block
        return carry

    lax.fori_loop(0, groups, unpack, 0)

    def finish(r, carry):
        b = r & (boxes - 1)
        p = r // boxes
        out_ref[b, p] = (dot_nt(eye_unknown, turned[r]) + near_sum[b, p]).astype(bf16)
        return carry

    lax.fori_loop(0, rows, finish, 0)

    sent = pl.ds(0, (n - 1) * 16)
    pltpu.make_async_copy(out1.at[sent], in1.at[sent], send1).wait()
    pltpu.make_async_copy(out2.at[sent], in2.at[sent], send2).wait()
    to_right.wait_send()
    to_left.wait_send()


def local(n, dirs, currents, near_blocks, near_mask, aggregate, disaggregate, centers):
    boxes, _, nu, angles = currents.shape
    dir_count = aggregate.shape[1]
    total = n * boxes
    f32, bf16 = jnp.float32, jnp.bfloat16
    vmem = pl.BlockSpec(memory_space=pltpu.VMEM)
    return pl.pallas_call(
        functools.partial(kernel, n, dirs),
        out_shape=jax.ShapeDtypeStruct(currents.shape, bf16),
        in_specs=[
            vmem,
            pl.BlockSpec(memory_space=pl.ANY),
            vmem,
            pl.BlockSpec(memory_space=pltpu.SMEM),
            vmem,
            vmem,
            vmem,
            vmem,
        ],
        out_specs=vmem,
        scratch_shapes=[
            pltpu.VMEM(near_blocks.shape, bf16),
            pltpu.SemaphoreType.DMA,
            pltpu.VMEM((2, 2, nu, angles), bf16),
            pltpu.SemaphoreType.DMA((2,)),
            pltpu.SemaphoreType.DMA((2,)),
            pltpu.VMEM((2 * boxes, angles, nu), bf16),
            pltpu.VMEM((n * 16, nu), bf16),
            pltpu.VMEM((n * 16, nu), bf16),
            pltpu.SemaphoreType.DMA,
            pltpu.SemaphoreType.DMA((n // 16,)),
            pltpu.VMEM((total, 8), f32),
            pltpu.VMEM((total, dir_count), f32),
            pltpu.VMEM((total, dir_count), f32),
            pltpu.VMEM((total, total), bf16),
            pltpu.VMEM((total, 2 * dir_count), bf16),
            pltpu.VMEM((n * 16, nu), bf16),
            pltpu.VMEM((n * 16, nu), bf16),
            pltpu.SemaphoreType.DMA,
            pltpu.SemaphoreType.DMA((n // 16,)),
            pltpu.VMEM((boxes + 2, nu, 2 * angles), bf16),
            pltpu.VMEM((boxes, 2, nu, angles), f32),
        ],
        compiler_params=pltpu.CompilerParams(
            collective_id=0, has_side_effects=True, vmem_limit_bytes=56 * 1024 * 1024
        ),
    )(
        currents,
        near_blocks,
        near_mask,
        near_mask,
        aggregate.reshape(2 * dir_count, nu),
        disaggregate.reshape(2 * nu, dir_count),
        centers,
        jnp.asarray(direction_turns(dir_count)),
    )


def solution(mesh):
    dirs = mesh.shape["dir"]
    return jax.shard_map(
        functools.partial(local, mesh.shape["box"] * dirs, dirs),
        mesh=mesh,
        in_specs=(
            P(("box", "dir"), None, None, None),
            P(("box", "dir"), None, None, None, None),
            P(),
            P(),
            P(),
            P(),
        ),
        out_specs=P(("box", "dir"), None, None, None),
        check_vma=False,
    )
```

```python
import functools
import math

import jax
import jax.numpy as jnp
import numpy as np
from jax import lax
from jax.experimental import pallas as pl
from jax.experimental.pallas import tpu as pltpu
from jax.sharding import PartitionSpec as P

MESH = pl.DeviceIdType.MESH
golden_turn = 2.399963229728653
far_gain = 8.0

COS_TERMS = (
    1.0,
    -19.73920440673828,
    64.93911743164062,
    -85.45014190673828,
    60.16762924194336,
    -25.967599868774414,
    6.528658390045166,
)
SIN_TERMS = (
    6.2831854820251465,
    -41.34170150756836,
    81.60513305664062,
    -76.70301818847656,
    42.02592849731445,
    -14.899847030639648,
    3.2381374835968018,
)


def polynomial(terms, x):
    total = x * terms[-1] + terms[-2]
    for term in terms[-3::-1]:
        total = total * x + term
    return total


def direction_turns(count):
    order = np.arange(count, dtype=np.float32)
    height = np.float32(1.0) - (np.float32(2.0) * order + np.float32(1.0)) / np.float32(count)
    radial = np.sqrt(np.float32(1.0) - height * height)
    azimuth = (order * np.float32(golden_turn)).astype(np.float64)
    rows = [radial * np.cos(azimuth), radial * np.sin(azimuth), height.astype(np.float64)]
    table = np.zeros((8, count), np.float32)
    for row, values in enumerate(rows):
        table[row] = (values / math.pi).astype(np.float32)
    return table


def dot_nt(left, right):
    return lax.dot_general(left, right, (((1,), (1,)), ((), ())), preferred_element_type=jnp.float32)


def dot_nn(left, right):
    return jnp.dot(left, right, preferred_element_type=jnp.float32)


def kernel(
    n,
    dirs,
    cur_ref,
    near_hbm,
    mask_ref,
    mask_smem,
    agg_ref,
    dis_ref,
    cen_ref,
    turn_ref,
    out_ref,
    near_v,
    near_sem,
    halo,
    halo_send,
    halo_recv,
    turned,
    out1,
    in1,
    send1,
    recv1,
    columns,
    cos_t,
    sin_t,
    trans,
    pattern,
    out2,
    in2,
    send2,
    recv2,
    padded,
    near_sum,
):
    f32, bf16 = jnp.float32, jnp.bfloat16
    boxes, _, nu, angles = cur_ref.shape
    rows = 2 * boxes
    total = n * boxes
    dir_count = agg_ref.shape[0] // 2
    groups = n // 16
    me = lax.axis_index("box") * dirs + lax.axis_index("dir")

    def place(device):
        return (device // dirs, lax.rem(device, dirs))

    fetch_near = pltpu.make_async_copy(near_hbm, near_v, near_sem)
    fetch_near.start()

    barrier = pltpu.get_barrier_semaphore()

    def greet(step, carry):
        pl.semaphore_signal(
            barrier, inc=1, device_id=place(lax.rem(me + step, n)), device_id_type=MESH
        )
        return carry

    lax.fori_loop(1, n, greet, 0)

    def equal(shape, row_of, col_of):
        row = lax.broadcasted_iota(jnp.int32, shape, 0)
        col = lax.broadcasted_iota(jnp.int32, shape, 1)
        return jnp.where(row_of(row) == col_of(col), 1.0, 0.0).astype(bf16)

    eye_angle = equal((angles, angles), lambda r: r, lambda c: c)
    eye_unknown = equal((nu, nu), lambda r: r, lambda c: c)
    swap = equal((256, 256), lambda r: r, lambda c: (c & 15) * 16 + (c >> 4))

    def turn(r, carry):
        block = cur_ref[r & (boxes - 1), r // boxes]
        turned[r] = dot_nt(eye_angle, block).astype(bf16)
        return carry

    lax.fori_loop(0, rows, turn, 0, unroll=4)

    def pack(g, carry):
        first = pl.multiple_of(g * 16, 16)
        block = turned[:, pl.ds(first, 16), :].reshape(256, nu)
        out1[pl.ds(pl.multiple_of(g * 256, 256), 256), :] = dot_nn(swap, block).astype(bf16)
        return carry

    lax.fori_loop(0, groups, pack, 0)

    pl.semaphore_wait(barrier, n - 1)

    def slot(device):
        return pl.ds(pl.multiple_of(device * 16, 16), 16)

    def send_out1(step, carry):
        device = lax.rem(me + step, n)
        pltpu.make_async_remote_copy(
            src_ref=out1.at[slot(device)],
            dst_ref=in1.at[slot(me)],
            send_sem=send1,
            recv_sem=recv1.at[me // 16],
            device_id=place(device),
            device_id_type=MESH,
        ).start()
        return carry

    lax.fori_loop(1, n, send_out1, 0)
    pltpu.make_async_copy(out1.at[slot(me)], in1.at[slot(me)], recv1.at[me // 16]).start()

    to_right = pltpu.make_async_remote_copy(
        src_ref=cur_ref.at[boxes - 1],
        dst_ref=halo.at[0],
        send_sem=halo_send.at[0],
        recv_sem=halo_recv.at[0],
        device_id=place(lax.rem(me + 1, n)),
        device_id_type=MESH,
    )
    to_left = pltpu.make_async_remote_copy(
        src_ref=cur_ref.at[0],
        dst_ref=halo.at[1],
        send_sem=halo_send.at[1],
        recv_sem=halo_recv.at[1],
        device_id=place(lax.rem(me + n - 1, n)),
        device_id_type=MESH,
    )
    to_right.start()
    to_left.start()

    low_row = 0.0 - mask_ref[0:1, :].astype(f32)
    high_row = mask_ref[1:2, :].astype(f32)
    table = jnp.concatenate(
        [cen_ref[...], low_row, high_row, jnp.zeros((3, total), f32)], axis=0
    )
    columns[...] = jnp.transpose(table)

    def phase(step, carry):
        own = pl.ds(pl.multiple_of(step * 16, 16), 16)
        block = columns[own, :]
        turns = (
            block[:, 0:1] * turn_ref[0:1, :]
            + block[:, 1:2] * turn_ref[1:2, :]
            + block[:, 2:3] * turn_ref[2:3, :]
        )
        rest = turns - jnp.round(turns)
        square = rest * rest
        cos_t[own, :] = polynomial(COS_TERMS, square)
        sin_t[own, :] = rest * polynomial(SIN_TERMS, square)
        return carry

    lax.fori_loop(0, total // 16, phase, 0, unroll=4)

    scale = far_gain / math.sqrt(total)

    def translation(step, carry):
        first = pl.multiple_of(step * 16, 16)
        block = columns[pl.ds(first, 16), :]
        row = (lax.broadcasted_iota(jnp.int32, (16, 1), 0) + first).astype(f32)
        low = row + block[:, 3:4]
        high = row + block[:, 4:5]
        for part in range(2):
            wide = slice(part * (total // 2), (part + 1) * (total // 2))
            squared = jnp.ones((16, total // 2), f32)
            for axis in range(3):
                spread = block[:, axis : axis + 1] - cen_ref[axis : axis + 1, wide]
                squared = squared + spread * spread
            spacing = squared * lax.rsqrt(squared)
            turns = spacing * (1.0 / math.pi)
            rest = turns - jnp.round(turns)
            value = polynomial(tuple(scale * t for t in COS_TERMS), rest * rest) / (1.0 + spacing)
            col = (
                lax.broadcasted_iota(jnp.int32, (1, total // 2), 1) + part * (total // 2)
            ).astype(f32)
            linked = (col >= low) & (col <= high)
            trans[pl.ds(first, 16), wide] = jnp.where(linked, 0.0, value).astype(bf16)
        return carry

    lax.fori_loop(0, total // 16, translation, 0, unroll=4)

    def gather(step, carry):
        g = lax.rem(me // 16 + groups - 1 - step, groups)
        span = pl.ds(pl.multiple_of(g * 256, 256), 256)
        pltpu.make_async_copy(in1.at[span], in1.at[span], recv1.at[g]).wait()
        product = dot_nt(in1[span, :], agg_ref[...]).reshape(16, 2, 8, 2 * dir_count)
        real = product[:, 0].reshape(128, 2 * dir_count)
        imag = product[:, 1].reshape(128, 2 * dir_count)
        pat_re = real[:, :dir_count] - imag[:, dir_count:]
        pat_im = real[:, dir_count:] + imag[:, :dir_count]
        own = pl.ds(pl.multiple_of(g * 128, 128), 128)
        cosine = cos_t[own, :]
        sine = sin_t[own, :]
        pattern[own, :dir_count] = (cosine * pat_re + sine * pat_im).astype(bf16)
        pattern[own, dir_count:] = (cosine * pat_im - sine * pat_re).astype(bf16)
        return carry

    lax.fori_loop(0, groups, gather, 0)

    def spread(step, carry):
        q = lax.rem(me // 32 + step, n // 32)
        own = pl.ds(pl.multiple_of(q * 256, 256), 256)
        summed = dot_nn(trans[own, :], pattern[...])
        sum_re = summed[:, :dir_count]
        sum_im = summed[:, dir_count:]
        cosine = cos_t[own, :]
        sine = sin_t[own, :]
        rec_re = (cosine * sum_re - sine * sum_im).astype(bf16)
        rec_im = (cosine * sum_im + sine * sum_re).astype(bf16)
        from_re = dot_nt(rec_re, dis_ref[...])
        from_im = dot_nt(rec_im, dis_ref[...])
        far_re = from_re[:, :nu] - from_im[:, nu:]
        far_im = from_im[:, :nu] + from_re[:, nu:]
        both = jnp.concatenate(
            [far_re.reshape(32, 1, 8, nu), far_im.reshape(32, 1, 8, nu)], axis=1
        ).reshape(512, nu)
        out2[pl.ds(pl.multiple_of(q * 512, 512), 512), :] = both.astype(bf16)

        def send_out2(k, inner):
            device = q * 32 + lax.rem(me + k, 32)

            @pl.when(device != me)
            def _():
                pltpu.make_async_remote_copy(
                    src_ref=out2.at[slot(device)],
                    dst_ref=in2.at[slot(me)],
                    send_sem=send2,
                    recv_sem=recv2.at[me // 16],
                    device_id=place(device),
                    device_id_type=MESH,
                ).start()

            return inner

        lax.fori_loop(0, 32, send_out2, 0)
        return carry

    lax.fori_loop(0, n // 32, spread, 0)
    pltpu.make_async_copy(out2.at[slot(me)], in2.at[slot(me)], recv2.at[me // 16]).start()

    to_right.wait_recv()
    to_left.wait_recv()
    padded[0, :, :angles] = halo[0, 0]
    padded[0, :, angles:] = halo[0, 1]
    padded[boxes + 1, :, :angles] = halo[1, 0]
    padded[boxes + 1, :, angles:] = halo[1, 1]

    def widen(b, carry):
        padded[b + 1, :, :angles] = cur_ref[b, 0]
        padded[b + 1, :, angles:] = cur_ref[b, 1]
        return carry

    lax.fori_loop(0, boxes, widen, 0)
    fetch_near.wait()

    def near(b, carry):
        box = me * boxes + b
        left = jnp.where(box > 0, mask_smem[0, box], 0).astype(f32)
        right = jnp.where(box < total - 1, mask_smem[1, box], 0).astype(f32)
        sides = []
        for part in range(2):
            sides.append(
                dot_nn(near_v[b, 0, part], padded[b + 1])
                + left * dot_nn(near_v[b, 1, part], padded[b])
                + right * dot_nn(near_v[b, 2, part], padded[b + 2])
            )
        near_sum[b, 0] = sides[0][:, :angles] - sides[1][:, angles:]
        near_sum[b, 1] = sides[0][:, angles:] + sides[1][:, :angles]
        return carry

    lax.fori_loop(0, boxes, near, 0, unroll=2)

    def unpack(step, carry):
        g = lax.rem(me // 16 + groups - 1 - step, groups)
        span = pl.ds(pl.multiple_of(g * 256, 256), 256)
        pltpu.make_async_copy(in2.at[span], in2.at[span], recv2.at[g]).wait()
        block = dot_nn(swap, in2[span, :]).astype(bf16).reshape(rows, 16, nu)
        turned[:, pl.ds(pl.multiple_of(g * 16, 16), 16), :] = block
        return carry

    lax.fori_loop(0, groups, unpack, 0)

    def finish(r, carry):
        b = r & (boxes - 1)
        p = r // boxes
        out_ref[b, p] = (dot_nt(eye_unknown, turned[r]) + near_sum[b, p]).astype(bf16)
        return carry

    lax.fori_loop(0, rows, finish, 0, unroll=8)

    sent = pl.ds(0, (n - 1) * 16)
    pltpu.make_async_copy(out1.at[sent], in1.at[sent], send1).wait()
    pltpu.make_async_copy(out2.at[sent], in2.at[sent], send2).wait()
    to_right.wait_send()
    to_left.wait_send()


def local(n, dirs, currents, near_blocks, near_mask, aggregate, disaggregate, centers):
    boxes, _, nu, angles = currents.shape
    dir_count = aggregate.shape[1]
    total = n * boxes
    f32, bf16 = jnp.float32, jnp.bfloat16
    vmem = pl.BlockSpec(memory_space=pltpu.VMEM)
    return pl.pallas_call(
        functools.partial(kernel, n, dirs),
        out_shape=pltpu.VMEM(currents.shape, bf16),
        in_specs=[
            vmem,
            pl.BlockSpec(memory_space=pl.ANY),
            vmem,
            pl.BlockSpec(memory_space=pltpu.SMEM),
            vmem,
            vmem,
            vmem,
            vmem,
        ],
        out_specs=vmem,
        scratch_shapes=[
            pltpu.VMEM(near_blocks.shape, bf16),
            pltpu.SemaphoreType.DMA,
            pltpu.VMEM((2, 2, nu, angles), bf16),
            pltpu.SemaphoreType.DMA((2,)),
            pltpu.SemaphoreType.DMA((2,)),
            pltpu.VMEM((2 * boxes, angles, nu), bf16),
            pltpu.VMEM((n * 16, nu), bf16),
            pltpu.VMEM((n * 16, nu), bf16),
            pltpu.SemaphoreType.DMA,
            pltpu.SemaphoreType.DMA((n // 16,)),
            pltpu.VMEM((total, 8), f32),
            pltpu.VMEM((total, dir_count), f32),
            pltpu.VMEM((total, dir_count), f32),
            pltpu.VMEM((total, total), bf16),
            pltpu.VMEM((total, 2 * dir_count), bf16),
            pltpu.VMEM((n * 16, nu), bf16),
            pltpu.VMEM((n * 16, nu), bf16),
            pltpu.SemaphoreType.DMA,
            pltpu.SemaphoreType.DMA((n // 16,)),
            pltpu.VMEM((boxes + 2, nu, 2 * angles), bf16),
            pltpu.VMEM((boxes, 2, nu, angles), f32),
        ],
        compiler_params=pltpu.CompilerParams(
            collective_id=0, has_side_effects=True, vmem_limit_bytes=56 * 1024 * 1024
        ),
    )(
        currents,
        near_blocks,
        near_mask,
        near_mask,
        aggregate.reshape(2 * dir_count, nu),
        disaggregate.reshape(2 * nu, dir_count),
        centers,
        jnp.asarray(direction_turns(dir_count)),
    )


def solution(mesh):
    dirs = mesh.shape["dir"]
    return jax.shard_map(
        functools.partial(local, mesh.shape["box"] * dirs, dirs),
        mesh=mesh,
        in_specs=(
            P(("box", "dir"), None, None, None),
            P(("box", "dir"), None, None, None, None),
            P(),
            P(),
            P(),
            P(),
        ),
        out_specs=P(("box", "dir"), None, None, None),
        check_vma=False,
    )
```

```python
import functools
import math

import jax
import jax.numpy as jnp
import numpy as np
from jax import lax
from jax.experimental import pallas as pl
from jax.experimental.pallas import tpu as pltpu
from jax.sharding import PartitionSpec as P

MESH = pl.DeviceIdType.MESH
golden_turn = 2.399963229728653
far_gain = 8.0

COS_TERMS = (
    1.0,
    -19.73920440673828,
    64.93911743164062,
    -85.45014190673828,
    60.16762924194336,
    -25.967599868774414,
    6.528658390045166,
)
SIN_TERMS = (
    6.2831854820251465,
    -41.34170150756836,
    81.60513305664062,
    -76.70301818847656,
    42.02592849731445,
    -14.899847030639648,
    3.2381374835968018,
)


def polynomial(terms, x):
    total = x * terms[-1] + terms[-2]
    for term in terms[-3::-1]:
        total = total * x + term
    return total


def direction_turns(count):
    order = np.arange(count, dtype=np.float32)
    height = np.float32(1.0) - (np.float32(2.0) * order + np.float32(1.0)) / np.float32(count)
    radial = np.sqrt(np.float32(1.0) - height * height)
    azimuth = (order * np.float32(golden_turn)).astype(np.float64)
    rows = [radial * np.cos(azimuth), radial * np.sin(azimuth), height.astype(np.float64)]
    table = np.zeros((8, count), np.float32)
    for row, values in enumerate(rows):
        table[row] = (values / math.pi).astype(np.float32)
    return table


def dot_nt(left, right):
    return lax.dot_general(left, right, (((1,), (1,)), ((), ())), preferred_element_type=jnp.float32)


def dot_nn(left, right):
    return jnp.dot(left, right, preferred_element_type=jnp.float32)


def kernel(
    n,
    dirs,
    cur_hbm,
    near_hbm,
    mask_ref,
    mask_smem,
    agg_hbm,
    dis_hbm,
    cen_ref,
    turn_ref,
    out_ref,
    cur_ref,
    agg_ref,
    dis_ref,
    near_v,
    fetch_sem,
    halo,
    halo_send,
    halo_recv,
    turned,
    out1,
    in1,
    send1,
    recv1,
    columns,
    ordered,
    ordered_rows,
    cos_t,
    sin_t,
    trans,
    pattern,
    out2,
    in2,
    send2,
    recv2,
    padded,
    near_sum,
):
    f32, bf16 = jnp.float32, jnp.bfloat16
    boxes, _, nu, angles = cur_ref.shape
    rows = 2 * boxes
    total = n * boxes
    dir_count = agg_ref.shape[0] // 2
    groups = n // 16
    me = lax.axis_index("box") * dirs + lax.axis_index("dir")

    def place(device):
        return (device // dirs, lax.rem(device, dirs))

    fetch_cur = pltpu.make_async_copy(cur_hbm, cur_ref, fetch_sem.at[0])
    fetch_agg = pltpu.make_async_copy(agg_hbm, agg_ref, fetch_sem.at[1])
    fetch_dis = pltpu.make_async_copy(dis_hbm, dis_ref, fetch_sem.at[2])
    fetch_near = pltpu.make_async_copy(near_hbm, near_v, fetch_sem.at[3])
    fetch_cur.start()

    barrier = pltpu.get_barrier_semaphore()

    def greet(step):
        pl.semaphore_signal(
            barrier, inc=1, device_id=place(lax.rem(me + step, n)), device_id_type=MESH
        )

    alone = (n - 1) - rows * 6

    def greet_alone(step, carry):
        greet(step + 1)
        return carry

    lax.fori_loop(0, alone, greet_alone, 0)

    def equal(shape, row_of, col_of):
        row = lax.broadcasted_iota(jnp.int32, shape, 0)
        col = lax.broadcasted_iota(jnp.int32, shape, 1)
        return jnp.where(row_of(row) == col_of(col), 1.0, 0.0).astype(bf16)

    eye_angle = equal((angles, angles), lambda r: r, lambda c: c)
    eye_unknown = equal((nu, nu), lambda r: r, lambda c: c)
    swap = equal((256, 256), lambda r: r, lambda c: (c & 15) * 16 + (c >> 4))

    fetch_cur.wait()
    fetch_agg.start()
    fetch_dis.start()
    fetch_near.start()

    def turn(r, carry):
        for k in range(6):
            greet(alone + 1 + r * 6 + k)
        block = cur_ref[r & (boxes - 1), r // boxes]
        turned[r] = dot_nt(eye_angle, block).astype(bf16)
        return carry

    lax.fori_loop(0, rows, turn, 0, unroll=4)

    def pack(g, carry):
        first = pl.multiple_of(g * 16, 16)
        block = turned[:, pl.ds(first, 16), :].reshape(256, nu)
        out1[pl.ds(pl.multiple_of(g * 256, 256), 256), :] = dot_nn(swap, block).astype(bf16)
        return carry

    lax.fori_loop(0, groups, pack, 0, unroll=4)

    pl.semaphore_wait(barrier, n - 1)

    my_high = ((me >> 4) & 4) | ((me >> 2) & 2) | ((me >> 1) & 1)
    my_low = ((me >> 2) & 12) | ((me >> 1) & 2) | (me & 1)

    def flip(i):
        return jnp.where((i & 1) == 0, i >> 1, 7 - (i >> 1))

    def spread_high(high):
        return ((high & 4) << 4) | ((high & 2) << 2) | ((high & 1) << 1)

    def spread_low(low):
        return ((low & 12) << 2) | ((low & 2) << 1) | (low & 1)

    def slot(position):
        return pl.ds(pl.multiple_of(position * 16, 16), 16)

    def send_out1(i, first):
        base = me ^ spread_high(flip(i))
        angle_base = (my_high ^ flip(i)) * 16
        for v in range(first, 16):
            pltpu.make_async_remote_copy(
                src_ref=out1.at[slot(angle_base + (my_low ^ v))],
                dst_ref=in1.at[slot(i * 16 + my_low)],
                send_sem=send1,
                recv_sem=recv1.at[i],
                device_id=place(base ^ spread_low(v)),
                device_id_type=MESH,
            ).start()

    send_out1(0, 1)

    def send_group(i, carry):
        send_out1(i, 0)
        return carry

    lax.fori_loop(1, groups, send_group, 0)
    pltpu.make_async_copy(
        out1.at[slot(my_high * 16 + my_low)], in1.at[slot(my_low)], recv1.at[0]
    ).start()

    to_right = pltpu.make_async_remote_copy(
        src_ref=cur_ref.at[boxes - 1],
        dst_ref=halo.at[0],
        send_sem=halo_send.at[0],
        recv_sem=halo_recv.at[0],
        device_id=place(lax.rem(me + 1, n)),
        device_id_type=MESH,
    )
    to_left = pltpu.make_async_remote_copy(
        src_ref=cur_ref.at[0],
        dst_ref=halo.at[1],
        send_sem=halo_send.at[1],
        recv_sem=halo_recv.at[1],
        device_id=place(lax.rem(me + n - 1, n)),
        device_id_type=MESH,
    )
    to_right.start()
    to_left.start()

    box_row = lax.broadcasted_iota(jnp.int32, (1, total), 1).astype(f32)
    low_row = box_row - mask_ref[0:1, :].astype(f32)
    high_row = box_row + mask_ref[1:2, :].astype(f32)
    table = jnp.concatenate(
        [cen_ref[...], low_row, high_row, box_row, jnp.zeros((2, total), f32)], axis=0
    )
    columns[...] = jnp.transpose(table)

    def order(i, carry):
        base = spread_high(my_high ^ flip(i))
        for low in range(16):
            source = pl.ds(pl.multiple_of((base | spread_low(low)) * 8, 8), 8)
            ordered[pl.ds(pl.multiple_of((i * 16 + low) * 8, 8), 8), :] = columns[source, :]
        return carry

    lax.fori_loop(0, groups, order, 0)
    ordered_rows[...] = jnp.transpose(ordered[...])

    def phase(step, carry):
        own = pl.ds(pl.multiple_of(step * 16, 16), 16)
        block = ordered[own, :]
        turns = (
            block[:, 0:1] * turn_ref[0:1, :]
            + block[:, 1:2] * turn_ref[1:2, :]
            + block[:, 2:3] * turn_ref[2:3, :]
        )
        rest = turns - jnp.round(turns)
        square = rest * rest
        cos_t[own, :] = polynomial(COS_TERMS, square)
        sin_t[own, :] = rest * polynomial(SIN_TERMS, square)
        return carry

    lax.fori_loop(0, total // 16, phase, 0, unroll=4)

    scale = far_gain / math.sqrt(total)

    def translation(step, carry):
        first = pl.multiple_of(step * 16, 16)
        block = ordered[pl.ds(first, 16), :]
        low = block[:, 3:4]
        high = block[:, 4:5]
        for part in range(2):
            wide = slice(part * (total // 2), (part + 1) * (total // 2))
            squared = jnp.ones((16, total // 2), f32)
            for axis in range(3):
                spread = block[:, axis : axis + 1] - ordered_rows[axis : axis + 1, wide]
                squared = squared + spread * spread
            spacing = squared * lax.rsqrt(squared)
            turns = spacing * (1.0 / math.pi)
            rest = turns - jnp.round(turns)
            value = polynomial(tuple(scale * t for t in COS_TERMS), rest * rest) / (1.0 + spacing)
            col = ordered_rows[5:6, wide]
            linked = (col >= low) & (col <= high)
            trans[pl.ds(first, 16), wide] = jnp.where(linked, 0.0, value).astype(bf16)
        return carry

    lax.fori_loop(0, total // 16, translation, 0, unroll=4)

    fetch_agg.wait()

    def gather(g, carry):
        span = pl.ds(pl.multiple_of(g * 256, 256), 256)
        pltpu.make_async_copy(in1.at[span], in1.at[span], recv1.at[g]).wait()
        product = dot_nt(in1[span, :], agg_ref[...]).reshape(16, 2, 8, 2 * dir_count)
        real = product[:, 0].reshape(128, 2 * dir_count)
        imag = product[:, 1].reshape(128, 2 * dir_count)
        pat_re = real[:, :dir_count] - imag[:, dir_count:]
        pat_im = real[:, dir_count:] + imag[:, :dir_count]
        own = pl.ds(pl.multiple_of(g * 128, 128), 128)
        cosine = cos_t[own, :]
        sine = sin_t[own, :]
        pattern[own, :dir_count] = (cosine * pat_re + sine * pat_im).astype(bf16)
        pattern[own, dir_count:] = (cosine * pat_im - sine * pat_re).astype(bf16)
        return carry

    lax.fori_loop(0, groups, gather, 0)

    fetch_dis.wait()

    def spread(q, carry):
        own = pl.ds(pl.multiple_of(q * 256, 256), 256)
        summed = dot_nn(trans[own, :], pattern[...])
        sum_re = summed[:, :dir_count]
        sum_im = summed[:, dir_count:]
        cosine = cos_t[own, :]
        sine = sin_t[own, :]
        rec_re = (cosine * sum_re - sine * sum_im).astype(bf16)
        rec_im = (cosine * sum_im + sine * sum_re).astype(bf16)
        from_re = dot_nt(rec_re, dis_ref[...])
        from_im = dot_nt(rec_im, dis_ref[...])
        far_re = from_re[:, :nu] - from_im[:, nu:]
        far_im = from_im[:, :nu] + from_re[:, nu:]
        both = jnp.concatenate(
            [far_re.reshape(32, 1, 8, nu), far_im.reshape(32, 1, 8, nu)], axis=1
        ).reshape(512, nu)
        out2[pl.ds(pl.multiple_of(q * 512, 512), 512), :] = both.astype(bf16)

        for half in range(2):
            i = q * 2 + half
            base = me ^ spread_high(flip(i))
            for v in range(16):
                copy = pltpu.make_async_remote_copy(
                    src_ref=out2.at[slot(i * 16 + (my_low ^ v))],
                    dst_ref=in2.at[slot(i * 16 + my_low)],
                    send_sem=send2,
                    recv_sem=recv2.at[i],
                    device_id=place(base ^ spread_low(v)),
                    device_id_type=MESH,
                )
                if half == 0 and v == 0:
                    pl.when(q > 0)(copy.start)
                else:
                    copy.start()
        return carry

    lax.fori_loop(0, n // 32, spread, 0)
    pltpu.make_async_copy(out2.at[slot(my_low)], in2.at[slot(my_low)], recv2.at[0]).start()

    to_right.wait_recv()
    to_left.wait_recv()
    padded[0, :, :angles] = halo[0, 0]
    padded[0, :, angles:] = halo[0, 1]
    padded[boxes + 1, :, :angles] = halo[1, 0]
    padded[boxes + 1, :, angles:] = halo[1, 1]

    def widen(b, carry):
        padded[b + 1, :, :angles] = cur_ref[b, 0]
        padded[b + 1, :, angles:] = cur_ref[b, 1]
        return carry

    lax.fori_loop(0, boxes, widen, 0)
    fetch_near.wait()

    def near(b, carry):
        box = me * boxes + b
        left = jnp.where(box > 0, mask_smem[0, box], 0).astype(f32)
        right = jnp.where(box < total - 1, mask_smem[1, box], 0).astype(f32)
        sides = []
        for part in range(2):
            sides.append(
                dot_nn(near_v[b, 0, part], padded[b + 1])
                + left * dot_nn(near_v[b, 1, part], padded[b])
                + right * dot_nn(near_v[b, 2, part], padded[b + 2])
            )
        near_sum[b, 0] = sides[0][:, :angles] - sides[1][:, angles:]
        near_sum[b, 1] = sides[0][:, angles:] + sides[1][:, :angles]
        return carry

    lax.fori_loop(0, boxes, near, 0, unroll=2)

    def unpack(g, carry):
        span = pl.ds(pl.multiple_of(g * 256, 256), 256)
        pltpu.make_async_copy(in2.at[span], in2.at[span], recv2.at[g]).wait()
        block = dot_nn(swap, in2[span, :]).astype(bf16).reshape(rows, 16, nu)
        turned[:, slot(my_high ^ flip(g)), :] = block
        return carry

    lax.fori_loop(0, groups, unpack, 0)

    def finish(pair, carry):
        far = dot_nt(eye_unknown, turned[pl.ds(pair * 2, 2)].reshape(2 * angles, nu))
        for k in range(2):
            r = pair * 2 + k
            b = r & (boxes - 1)
            p = r // boxes
            out_ref[b, p] = (far[:, k * angles : (k + 1) * angles] + near_sum[b, p]).astype(bf16)
        return carry

    lax.fori_loop(0, rows // 2, finish, 0, unroll=4)

    sent = pl.ds(0, (n - 1) * 16)
    pltpu.make_async_copy(out1.at[sent], in1.at[sent], send1).wait()
    pltpu.make_async_copy(out2.at[sent], in2.at[sent], send2).wait()
    to_right.wait_send()
    to_left.wait_send()


def local(n, dirs, currents, near_blocks, near_mask, aggregate, disaggregate, centers):
    boxes, _, nu, angles = currents.shape
    dir_count = aggregate.shape[1]
    total = n * boxes
    f32, bf16 = jnp.float32, jnp.bfloat16
    vmem = pl.BlockSpec(memory_space=pltpu.VMEM)
    anywhere = pl.BlockSpec(memory_space=pl.ANY)
    return pl.pallas_call(
        functools.partial(kernel, n, dirs),
        out_shape=pltpu.VMEM(currents.shape, bf16),
        in_specs=[
            anywhere,
            anywhere,
            vmem,
            pl.BlockSpec(memory_space=pltpu.SMEM),
            anywhere,
            anywhere,
            vmem,
            vmem,
        ],
        out_specs=vmem,
        scratch_shapes=[
            pltpu.VMEM(currents.shape, bf16),
            pltpu.VMEM((2 * dir_count, nu), bf16),
            pltpu.VMEM((2 * nu, dir_count), bf16),
            pltpu.VMEM(near_blocks.shape, bf16),
            pltpu.SemaphoreType.DMA((4,)),
            pltpu.VMEM((2, 2, nu, angles), bf16),
            pltpu.SemaphoreType.DMA((2,)),
            pltpu.SemaphoreType.DMA((2,)),
            pltpu.VMEM((2 * boxes, angles, nu), bf16),
            pltpu.VMEM((n * 16, nu), bf16),
            pltpu.VMEM((n * 16, nu), bf16),
            pltpu.SemaphoreType.DMA,
            pltpu.SemaphoreType.DMA((n // 16,)),
            pltpu.VMEM((total, 8), f32),
            pltpu.VMEM((total, 8), f32),
            pltpu.VMEM((8, total), f32),
            pltpu.VMEM((total, dir_count), f32),
            pltpu.VMEM((total, dir_count), f32),
            pltpu.VMEM((total, total), bf16),
            pltpu.VMEM((total, 2 * dir_count), bf16),
            pltpu.VMEM((n * 16, nu), bf16),
            pltpu.VMEM((n * 16, nu), bf16),
            pltpu.SemaphoreType.DMA,
            pltpu.SemaphoreType.DMA((n // 16,)),
            pltpu.VMEM((boxes + 2, nu, 2 * angles), bf16),
            pltpu.VMEM((boxes, 2, nu, angles), f32),
        ],
        compiler_params=pltpu.CompilerParams(
            collective_id=0, has_side_effects=True, vmem_limit_bytes=56 * 1024 * 1024
        ),
    )(
        currents,
        near_blocks,
        near_mask,
        near_mask,
        aggregate.reshape(2 * dir_count, nu),
        disaggregate.reshape(2 * nu, dir_count),
        centers,
        jnp.asarray(direction_turns(dir_count)),
    )


def solution(mesh):
    dirs = mesh.shape["dir"]
    return jax.shard_map(
        functools.partial(local, mesh.shape["box"] * dirs, dirs),
        mesh=mesh,
        in_specs=(
            P(("box", "dir"), None, None, None),
            P(("box", "dir"), None, None, None, None),
            P(),
            P(),
            P(),
            P(),
        ),
        out_specs=P(("box", "dir"), None, None, None),
        check_vma=False,
    )
```

```python
import functools
import math

import jax
import jax.numpy as jnp
import numpy as np
from jax import lax
from jax.experimental import pallas as pl
from jax.experimental.pallas import tpu as pltpu
from jax.sharding import PartitionSpec as P

MESH = pl.DeviceIdType.MESH
golden_turn = 2.399963229728653
far_gain = 8.0

COS_TERMS = (
    1.0,
    -19.73920440673828,
    64.93911743164062,
    -85.45014190673828,
    60.16762924194336,
    -25.967599868774414,
    6.528658390045166,
)
SIN_TERMS = (
    6.2831854820251465,
    -41.34170150756836,
    81.60513305664062,
    -76.70301818847656,
    42.02592849731445,
    -14.899847030639648,
    3.2381374835968018,
)


def polynomial(terms, x):
    total = x * terms[-1] + terms[-2]
    for term in terms[-3::-1]:
        total = total * x + term
    return total


def direction_turns(count):
    order = np.arange(count, dtype=np.float32)
    height = np.float32(1.0) - (np.float32(2.0) * order + np.float32(1.0)) / np.float32(count)
    radial = np.sqrt(np.float32(1.0) - height * height)
    azimuth = (order * np.float32(golden_turn)).astype(np.float64)
    rows = [radial * np.cos(azimuth), radial * np.sin(azimuth), height.astype(np.float64)]
    table = np.zeros((8, count), np.float32)
    for row, values in enumerate(rows):
        table[row] = (values / math.pi).astype(np.float32)
    return table


def dot_nt(left, right):
    return lax.dot_general(left, right, (((1,), (1,)), ((), ())), preferred_element_type=jnp.float32)


def dot_nn(left, right):
    return jnp.dot(left, right, preferred_element_type=jnp.float32)


def kernel(
    n,
    dirs,
    cur_hbm,
    near_hbm,
    mask_ref,
    mask_smem,
    agg_hbm,
    dis_hbm,
    cen_ref,
    turn_ref,
    out_ref,
    cur_ref,
    agg_ref,
    dis_ref,
    near_v,
    fetch_sem,
    halo,
    halo_send,
    halo_recv,
    turned,
    out1,
    in1,
    send1,
    recv1,
    columns,
    ordered,
    ordered_rows,
    cos_t,
    sin_t,
    trans,
    pattern,
    out2,
    in2,
    send2,
    recv2,
    padded,
    near_sum,
):
    f32, bf16 = jnp.float32, jnp.bfloat16
    boxes, _, nu, angles = cur_ref.shape
    rows = 2 * boxes
    total = n * boxes
    dir_count = agg_ref.shape[0] // 2
    groups = n // 16
    me = lax.axis_index("box") * dirs + lax.axis_index("dir")

    def place(device):
        return (device // dirs, lax.rem(device, dirs))

    fetch_cur = pltpu.make_async_copy(cur_hbm, cur_ref, fetch_sem.at[0])
    fetch_agg = pltpu.make_async_copy(agg_hbm, agg_ref, fetch_sem.at[1])
    fetch_dis = pltpu.make_async_copy(dis_hbm, dis_ref, fetch_sem.at[2])
    fetch_near = pltpu.make_async_copy(near_hbm, near_v, fetch_sem.at[3])
    fetch_cur.start()

    barrier = pltpu.get_barrier_semaphore()

    def greet(device):
        pl.semaphore_signal(barrier, inc=1, device_id=place(device), device_id_type=MESH)

    root = 122
    first = (me // 16) * 16 + 10

    @pl.when(me != root)
    def _():
        greet(root)

    def equal(shape, row_of, col_of):
        row = lax.broadcasted_iota(jnp.int32, shape, 0)
        col = lax.broadcasted_iota(jnp.int32, shape, 1)
        return jnp.where(row_of(row) == col_of(col), 1.0, 0.0).astype(bf16)

    eye_angle = equal((angles, angles), lambda r: r, lambda c: c)
    eye_unknown = equal((nu, nu), lambda r: r, lambda c: c)
    swap = equal((256, 256), lambda r: r, lambda c: (c & 15) * 16 + (c >> 4))

    fetch_cur.wait()
    fetch_agg.start()
    fetch_dis.start()
    fetch_near.start()

    def turn(r, carry):
        block = cur_ref[r & (boxes - 1), r // boxes]
        turned[r] = dot_nt(eye_angle, block).astype(bf16)
        return carry

    lax.fori_loop(0, rows, turn, 0, unroll=4)

    def pack(g, carry):
        first = pl.multiple_of(g * 16, 16)
        block = turned[:, pl.ds(first, 16), :].reshape(256, nu)
        out1[pl.ds(pl.multiple_of(g * 256, 256), 256), :] = dot_nn(swap, block).astype(bf16)
        return carry

    lax.fori_loop(0, groups, pack, 0, unroll=4)


    @pl.when(me == root)
    def _():
        pl.semaphore_wait(barrier, n - 1)
        for k in range(n // 16):
            if k * 16 + 10 != root:
                greet(k * 16 + 10)

    @pl.when(me != root)
    def _():
        pl.semaphore_wait(barrier, 1)

    @pl.when(me == first)
    def _():
        for k in range(16):
            if k != 10:
                greet((me // 16) * 16 + k)


    my_high = ((me >> 4) & 4) | ((me >> 2) & 2) | ((me >> 1) & 1)
    my_low = ((me >> 2) & 12) | ((me >> 1) & 2) | (me & 1)

    def flip(i):
        return jnp.where((i & 1) == 0, i >> 1, 7 - (i >> 1))

    def spread_high(high):
        return ((high & 4) << 4) | ((high & 2) << 2) | ((high & 1) << 1)

    def spread_low(low):
        return ((low & 12) << 2) | ((low & 2) << 1) | (low & 1)

    def slot(position):
        return pl.ds(pl.multiple_of(position * 16, 16), 16)

    def send_out1(i, first):
        base = me ^ spread_high(flip(i))
        angle_base = (my_high ^ flip(i)) * 16
        for v in range(first, 16):
            pltpu.make_async_remote_copy(
                src_ref=out1.at[slot(angle_base + (my_low ^ v))],
                dst_ref=in1.at[slot(i * 16 + my_low)],
                send_sem=send1,
                recv_sem=recv1.at[i],
                device_id=place(base ^ spread_low(v)),
                device_id_type=MESH,
            ).start()

    send_out1(0, 1)

    def send_group(i, carry):
        send_out1(i, 0)
        return carry

    lax.fori_loop(1, groups, send_group, 0)
    pltpu.make_async_copy(
        out1.at[slot(my_high * 16 + my_low)], in1.at[slot(my_low)], recv1.at[0]
    ).start()

    to_right = pltpu.make_async_remote_copy(
        src_ref=cur_ref.at[boxes - 1],
        dst_ref=halo.at[0],
        send_sem=halo_send.at[0],
        recv_sem=halo_recv.at[0],
        device_id=place(lax.rem(me + 1, n)),
        device_id_type=MESH,
    )
    to_left = pltpu.make_async_remote_copy(
        src_ref=cur_ref.at[0],
        dst_ref=halo.at[1],
        send_sem=halo_send.at[1],
        recv_sem=halo_recv.at[1],
        device_id=place(lax.rem(me + n - 1, n)),
        device_id_type=MESH,
    )
    to_right.start()
    to_left.start()

    box_row = lax.broadcasted_iota(jnp.int32, (1, total), 1).astype(f32)
    low_row = box_row - mask_ref[0:1, :].astype(f32)
    high_row = box_row + mask_ref[1:2, :].astype(f32)
    table = jnp.concatenate(
        [cen_ref[...], low_row, high_row, box_row, jnp.zeros((2, total), f32)], axis=0
    )
    columns[...] = jnp.transpose(table)

    def order(i, carry):
        base = spread_high(my_high ^ flip(i))
        for low in range(16):
            source = pl.ds(pl.multiple_of((base | spread_low(low)) * 8, 8), 8)
            ordered[pl.ds(pl.multiple_of((i * 16 + low) * 8, 8), 8), :] = columns[source, :]
        return carry

    lax.fori_loop(0, groups, order, 0)
    ordered_rows[...] = jnp.transpose(ordered[...])

    def phase(step, carry):
        own = pl.ds(pl.multiple_of(step * 16, 16), 16)
        block = ordered[own, :]
        turns = (
            block[:, 0:1] * turn_ref[0:1, :]
            + block[:, 1:2] * turn_ref[1:2, :]
            + block[:, 2:3] * turn_ref[2:3, :]
        )
        rest = turns - jnp.round(turns)
        square = rest * rest
        cos_t[own, :] = polynomial(COS_TERMS, square)
        sin_t[own, :] = rest * polynomial(SIN_TERMS, square)
        return carry

    lax.fori_loop(0, total // 16, phase, 0, unroll=4)

    scale = far_gain / math.sqrt(total)

    def translation(step, carry):
        first = pl.multiple_of(step * 16, 16)
        block = ordered[pl.ds(first, 16), :]
        low = block[:, 3:4]
        high = block[:, 4:5]
        for part in range(2):
            wide = slice(part * (total // 2), (part + 1) * (total // 2))
            squared = jnp.ones((16, total // 2), f32)
            for axis in range(3):
                spread = block[:, axis : axis + 1] - ordered_rows[axis : axis + 1, wide]
                squared = squared + spread * spread
            spacing = squared * lax.rsqrt(squared)
            turns = spacing * (1.0 / math.pi)
            rest = turns - jnp.round(turns)
            value = polynomial(tuple(scale * t for t in COS_TERMS), rest * rest) / (1.0 + spacing)
            col = ordered_rows[5:6, wide]
            linked = (col >= low) & (col <= high)
            trans[pl.ds(first, 16), wide] = jnp.where(linked, 0.0, value).astype(bf16)
        return carry

    lax.fori_loop(0, total // 16, translation, 0, unroll=4)

    fetch_agg.wait()

    def gather(g, carry):
        span = pl.ds(pl.multiple_of(g * 256, 256), 256)
        pltpu.make_async_copy(in1.at[span], in1.at[span], recv1.at[g]).wait()
        product = dot_nt(in1[span, :], agg_ref[...]).reshape(16, 2, 8, 2 * dir_count)
        real = product[:, 0].reshape(128, 2 * dir_count)
        imag = product[:, 1].reshape(128, 2 * dir_count)
        pat_re = real[:, :dir_count] - imag[:, dir_count:]
        pat_im = real[:, dir_count:] + imag[:, :dir_count]
        own = pl.ds(pl.multiple_of(g * 128, 128), 128)
        cosine = cos_t[own, :]
        sine = sin_t[own, :]
        pattern[own, :dir_count] = (cosine * pat_re + sine * pat_im).astype(bf16)
        pattern[own, dir_count:] = (cosine * pat_im - sine * pat_re).astype(bf16)
        return carry

    lax.fori_loop(0, groups, gather, 0)

    fetch_dis.wait()

    def spread(q, carry):
        own = pl.ds(pl.multiple_of(q * 256, 256), 256)
        summed = dot_nn(trans[own, :], pattern[...])
        sum_re = summed[:, :dir_count]
        sum_im = summed[:, dir_count:]
        cosine = cos_t[own, :]
        sine = sin_t[own, :]
        rec_re = (cosine * sum_re - sine * sum_im).astype(bf16)
        rec_im = (cosine * sum_im + sine * sum_re).astype(bf16)
        from_re = dot_nt(rec_re, dis_ref[...])
        from_im = dot_nt(rec_im, dis_ref[...])
        far_re = from_re[:, :nu] - from_im[:, nu:]
        far_im = from_im[:, :nu] + from_re[:, nu:]
        both = jnp.concatenate(
            [far_re.reshape(32, 1, 8, nu), far_im.reshape(32, 1, 8, nu)], axis=1
        ).reshape(512, nu)
        out2[pl.ds(pl.multiple_of(q * 512, 512), 512), :] = both.astype(bf16)

        for half in range(2):
            i = q * 2 + half
            base = me ^ spread_high(flip(i))
            for v in range(16):
                copy = pltpu.make_async_remote_copy(
                    src_ref=out2.at[slot(i * 16 + (my_low ^ v))],
                    dst_ref=in2.at[slot(i * 16 + my_low)],
                    send_sem=send2,
                    recv_sem=recv2.at[i],
                    device_id=place(base ^ spread_low(v)),
                    device_id_type=MESH,
                )
                if half == 0 and v == 0:
                    pl.when(q > 0)(copy.start)
                else:
                    copy.start()
        return carry

    lax.fori_loop(0, n // 32, spread, 0)
    pltpu.make_async_copy(out2.at[slot(my_low)], in2.at[slot(my_low)], recv2.at[0]).start()

    to_right.wait_recv()
    to_left.wait_recv()
    padded[0, :, :angles] = halo[0, 0]
    padded[0, :, angles:] = halo[0, 1]
    padded[boxes + 1, :, :angles] = halo[1, 0]
    padded[boxes + 1, :, angles:] = halo[1, 1]

    def widen(b, carry):
        padded[b + 1, :, :angles] = cur_ref[b, 0]
        padded[b + 1, :, angles:] = cur_ref[b, 1]
        return carry

    lax.fori_loop(0, boxes, widen, 0)
    fetch_near.wait()

    def near(b, carry):
        box = me * boxes + b
        left = jnp.where(box > 0, mask_smem[0, box], 0).astype(f32)
        right = jnp.where(box < total - 1, mask_smem[1, box], 0).astype(f32)
        sides = []
        for part in range(2):
            sides.append(
                dot_nn(near_v[b, 0, part], padded[b + 1])
                + left * dot_nn(near_v[b, 1, part], padded[b])
                + right * dot_nn(near_v[b, 2, part], padded[b + 2])
            )
        near_sum[b, 0] = sides[0][:, :angles] - sides[1][:, angles:]
        near_sum[b, 1] = sides[0][:, angles:] + sides[1][:, :angles]
        return carry

    lax.fori_loop(0, boxes, near, 0, unroll=2)

    def unpack(g, carry):
        span = pl.ds(pl.multiple_of(g * 256, 256), 256)
        pltpu.make_async_copy(in2.at[span], in2.at[span], recv2.at[g]).wait()
        block = dot_nn(swap, in2[span, :]).astype(bf16).reshape(rows, 16, nu)
        turned[:, slot(my_high ^ flip(g)), :] = block
        return carry

    lax.fori_loop(0, groups, unpack, 0)

    def finish(pair, carry):
        far = dot_nt(eye_unknown, turned[pl.ds(pair * 2, 2)].reshape(2 * angles, nu))
        for k in range(2):
            r = pair * 2 + k
            b = r & (boxes - 1)
            p = r // boxes
            out_ref[b, p] = (far[:, k * angles : (k + 1) * angles] + near_sum[b, p]).astype(bf16)
        return carry

    lax.fori_loop(0, rows // 2, finish, 0, unroll=4)

    sent = pl.ds(0, (n - 1) * 16)
    pltpu.make_async_copy(out1.at[sent], in1.at[sent], send1).wait()
    pltpu.make_async_copy(out2.at[sent], in2.at[sent], send2).wait()
    to_right.wait_send()
    to_left.wait_send()


def local(n, dirs, currents, near_blocks, near_mask, aggregate, disaggregate, centers):
    boxes, _, nu, angles = currents.shape
    dir_count = aggregate.shape[1]
    total = n * boxes
    f32, bf16 = jnp.float32, jnp.bfloat16
    vmem = pl.BlockSpec(memory_space=pltpu.VMEM)
    anywhere = pl.BlockSpec(memory_space=pl.ANY)
    return pl.pallas_call(
        functools.partial(kernel, n, dirs),
        out_shape=pltpu.VMEM(currents.shape, bf16),
        in_specs=[
            anywhere,
            anywhere,
            vmem,
            pl.BlockSpec(memory_space=pltpu.SMEM),
            anywhere,
            anywhere,
            vmem,
            vmem,
        ],
        out_specs=vmem,
        scratch_shapes=[
            pltpu.VMEM(currents.shape, bf16),
            pltpu.VMEM((2 * dir_count, nu), bf16),
            pltpu.VMEM((2 * nu, dir_count), bf16),
            pltpu.VMEM(near_blocks.shape, bf16),
            pltpu.SemaphoreType.DMA((4,)),
            pltpu.VMEM((2, 2, nu, angles), bf16),
            pltpu.SemaphoreType.DMA((2,)),
            pltpu.SemaphoreType.DMA((2,)),
            pltpu.VMEM((2 * boxes, angles, nu), bf16),
            pltpu.VMEM((n * 16, nu), bf16),
            pltpu.VMEM((n * 16, nu), bf16),
            pltpu.SemaphoreType.DMA,
            pltpu.SemaphoreType.DMA((n // 16,)),
            pltpu.VMEM((total, 8), f32),
            pltpu.VMEM((total, 8), f32),
            pltpu.VMEM((8, total), f32),
            pltpu.VMEM((total, dir_count), f32),
            pltpu.VMEM((total, dir_count), f32),
            pltpu.VMEM((total, total), bf16),
            pltpu.VMEM((total, 2 * dir_count), bf16),
            pltpu.VMEM((n * 16, nu), bf16),
            pltpu.VMEM((n * 16, nu), bf16),
            pltpu.SemaphoreType.DMA,
            pltpu.SemaphoreType.DMA((n // 16,)),
            pltpu.VMEM((boxes + 2, nu, 2 * angles), bf16),
            pltpu.VMEM((boxes, 2, nu, angles), f32),
        ],
        compiler_params=pltpu.CompilerParams(
            collective_id=0, has_side_effects=True, vmem_limit_bytes=56 * 1024 * 1024
        ),
    )(
        currents,
        near_blocks,
        near_mask,
        near_mask,
        aggregate.reshape(2 * dir_count, nu),
        disaggregate.reshape(2 * nu, dir_count),
        centers,
        jnp.asarray(direction_turns(dir_count)),
    )


def solution(mesh):
    dirs = mesh.shape["dir"]
    return jax.shard_map(
        functools.partial(local, mesh.shape["box"] * dirs, dirs),
        mesh=mesh,
        in_specs=(
            P(("box", "dir"), None, None, None),
            P(("box", "dir"), None, None, None, None),
            P(),
            P(),
            P(),
            P(),
        ),
        out_specs=P(("box", "dir"), None, None, None),
        check_vma=False,
    )
```

```python
import functools
import math

import jax
import jax.numpy as jnp
import numpy as np
from jax import lax
from jax.experimental import pallas as pl
from jax.experimental.pallas import tpu as pltpu
from jax.sharding import PartitionSpec as P

MESH = pl.DeviceIdType.MESH
golden_turn = 2.399963229728653
far_gain = 8.0

COS_TERMS = (
    1.0,
    -19.73920440673828,
    64.93911743164062,
    -85.45014190673828,
    60.16762924194336,
    -25.967599868774414,
    6.528658390045166,
)
SIN_TERMS = (
    6.2831854820251465,
    -41.34170150756836,
    81.60513305664062,
    -76.70301818847656,
    42.02592849731445,
    -14.899847030639648,
    3.2381374835968018,
)


def polynomial(terms, x):
    total = x * terms[-1] + terms[-2]
    for term in terms[-3::-1]:
        total = total * x + term
    return total


def direction_turns(count):
    order = np.arange(count, dtype=np.float32)
    height = np.float32(1.0) - (np.float32(2.0) * order + np.float32(1.0)) / np.float32(count)
    radial = np.sqrt(np.float32(1.0) - height * height)
    azimuth = (order * np.float32(golden_turn)).astype(np.float64)
    rows = [radial * np.cos(azimuth), radial * np.sin(azimuth), height.astype(np.float64)]
    table = np.zeros((8, count), np.float32)
    for row, values in enumerate(rows):
        table[row] = (values / math.pi).astype(np.float32)
    return table


def dot_nt(left, right):
    return lax.dot_general(left, right, (((1,), (1,)), ((), ())), preferred_element_type=jnp.float32)


def dot_nn(left, right):
    return jnp.dot(left, right, preferred_element_type=jnp.float32)


def kernel(
    n,
    dirs,
    cur_hbm,
    near_hbm,
    mask_hbm,
    agg_hbm,
    dis_hbm,
    cen_hbm,
    turn_hbm,
    out_ref,
    mask_ref,
    mask_smem,
    cen_ref,
    turn_ref,
    cur_ref,
    agg_ref,
    dis_ref,
    near_v,
    fetch_sem,
    halo,
    halo_send,
    halo_recv,
    turned,
    out1,
    in1,
    send1,
    recv1,
    columns,
    ordered,
    ordered_rows,
    cos_t,
    sin_t,
    trans,
    pattern,
    out2,
    in2,
    send2,
    recv2,
    padded,
    near_sum,
    partial,
):
    f32, bf16 = jnp.float32, jnp.bfloat16
    boxes, _, nu, angles = cur_ref.shape
    rows = 2 * boxes
    total = n * boxes
    dir_count = agg_ref.shape[0] // 2
    groups = n // 16
    me = lax.axis_index("box") * dirs + lax.axis_index("dir")

    def place(device):
        return (device // dirs, lax.rem(device, dirs))

    fetch_cur = pltpu.make_async_copy(cur_hbm, cur_ref, fetch_sem.at[0])
    fetch_agg = pltpu.make_async_copy(agg_hbm, agg_ref, fetch_sem.at[1])
    fetch_dis = pltpu.make_async_copy(dis_hbm, dis_ref, fetch_sem.at[2])
    fetch_near = pltpu.make_async_copy(near_hbm, near_v, fetch_sem.at[3])
    small = [
        pltpu.make_async_copy(cen_hbm, cen_ref, fetch_sem.at[4]),
        pltpu.make_async_copy(turn_hbm, turn_ref, fetch_sem.at[5]),
        pltpu.make_async_copy(mask_hbm, mask_ref, fetch_sem.at[6]),
        pltpu.make_async_copy(mask_hbm, mask_smem, fetch_sem.at[7]),
    ]
    fetch_cur.start()

    barrier = pltpu.get_barrier_semaphore()

    def greet(device):
        pl.semaphore_signal(barrier, inc=1, device_id=place(device), device_id_type=MESH)

    root = 122
    first = (me // 16) * 16 + 10

    @pl.when(me != root)
    def _():
        greet(root)

    def equal(shape, row_of, col_of):
        row = lax.broadcasted_iota(jnp.int32, shape, 0)
        col = lax.broadcasted_iota(jnp.int32, shape, 1)
        return jnp.where(row_of(row) == col_of(col), 1.0, 0.0).astype(bf16)

    eye_angle = equal((angles, angles), lambda r: r, lambda c: c)
    eye_unknown = equal((nu, nu), lambda r: r, lambda c: c)
    swap = equal((256, 256), lambda r: r, lambda c: (c & 15) * 16 + (c >> 4))

    fetch_cur.wait()
    fetch_agg.start()
    fetch_dis.start()
    fetch_near.start()
    for copy in small:
        copy.start()

    def turn(r, carry):
        block = cur_ref[r & (boxes - 1), r // boxes]
        turned[r] = dot_nt(eye_angle, block).astype(bf16)
        return carry

    lax.fori_loop(0, rows, turn, 0, unroll=4)

    def pack(g, carry):
        first = pl.multiple_of(g * 16, 16)
        block = turned[:, pl.ds(first, 16), :].reshape(256, nu)
        out1[pl.ds(pl.multiple_of(g * 256, 256), 256), :] = dot_nn(swap, block).astype(bf16)
        return carry

    lax.fori_loop(0, groups, pack, 0, unroll=4)


    @pl.when(me == root)
    def _():
        pl.semaphore_wait(barrier, n - 1)
        for k in range(n // 16):
            if k * 16 + 10 != root:
                greet(k * 16 + 10)

    @pl.when(me != root)
    def _():
        pl.semaphore_wait(barrier, 1)

    @pl.when(me == first)
    def _():
        for k in range(16):
            if k != 10:
                greet((me // 16) * 16 + k)


    my_high = ((me >> 4) & 4) | ((me >> 2) & 2) | ((me >> 1) & 1)
    my_low = ((me >> 2) & 12) | ((me >> 1) & 2) | (me & 1)

    def flip(i):
        return jnp.where((i & 1) == 0, i >> 1, 7 - (i >> 1))

    def spread_high(high):
        return ((high & 4) << 4) | ((high & 2) << 2) | ((high & 1) << 1)

    def spread_low(low):
        return ((low & 12) << 2) | ((low & 2) << 1) | (low & 1)

    def slot(position):
        return pl.ds(pl.multiple_of(position * 16, 16), 16)

    def send_out1(i, first):
        base = me ^ spread_high(flip(i))
        angle_base = (my_high ^ flip(i)) * 16
        for v in range(first, 16):
            pltpu.make_async_remote_copy(
                src_ref=out1.at[slot(angle_base + (my_low ^ v))],
                dst_ref=in1.at[slot(i * 16 + my_low)],
                send_sem=send1,
                recv_sem=recv1.at[i],
                device_id=place(base ^ spread_low(v)),
                device_id_type=MESH,
            ).start()

    send_out1(0, 1)

    def send_group(i, carry):
        send_out1(i, 0)
        return carry

    lax.fori_loop(1, groups, send_group, 0)
    pltpu.make_async_copy(
        out1.at[slot(my_high * 16 + my_low)], in1.at[slot(my_low)], recv1.at[0]
    ).start()

    to_right = pltpu.make_async_remote_copy(
        src_ref=cur_ref.at[boxes - 1],
        dst_ref=halo.at[0],
        send_sem=halo_send.at[0],
        recv_sem=halo_recv.at[0],
        device_id=place(lax.rem(me + 1, n)),
        device_id_type=MESH,
    )
    to_left = pltpu.make_async_remote_copy(
        src_ref=cur_ref.at[0],
        dst_ref=halo.at[1],
        send_sem=halo_send.at[1],
        recv_sem=halo_recv.at[1],
        device_id=place(lax.rem(me + n - 1, n)),
        device_id_type=MESH,
    )
    to_right.start()
    to_left.start()

    for copy in small:
        copy.wait()

    box_row = lax.broadcasted_iota(jnp.int32, (1, total), 1).astype(f32)
    low_row = box_row - mask_ref[0:1, :].astype(f32)
    high_row = box_row + mask_ref[1:2, :].astype(f32)
    table = jnp.concatenate(
        [cen_ref[...], low_row, high_row, box_row, jnp.zeros((2, total), f32)], axis=0
    )
    columns[...] = jnp.transpose(table)

    def order(i, carry):
        base = spread_high(my_high ^ flip(i))
        for low in range(16):
            source = pl.ds(pl.multiple_of((base | spread_low(low)) * 8, 8), 8)
            ordered[pl.ds(pl.multiple_of((i * 16 + low) * 8, 8), 8), :] = columns[source, :]
        return carry

    lax.fori_loop(0, groups, order, 0)
    ordered_rows[...] = jnp.transpose(ordered[...])

    def phase(step, carry):
        own = pl.ds(pl.multiple_of(step * 16, 16), 16)
        block = ordered[own, :]
        turns = (
            block[:, 0:1] * turn_ref[0:1, :]
            + block[:, 1:2] * turn_ref[1:2, :]
            + block[:, 2:3] * turn_ref[2:3, :]
        )
        rest = turns - jnp.round(turns)
        square = rest * rest
        cos_t[own, :] = polynomial(COS_TERMS, square)
        sin_t[own, :] = rest * polynomial(SIN_TERMS, square)
        return carry

    lax.fori_loop(0, total // 16, phase, 0, unroll=4)

    scale = far_gain / math.sqrt(total)

    def translation(step, carry):
        first = pl.multiple_of(step * 16, 16)
        block = ordered[pl.ds(first, 16), :]
        low = block[:, 3:4]
        high = block[:, 4:5]
        for part in range(2):
            wide = slice(part * (total // 2), (part + 1) * (total // 2))
            squared = jnp.ones((16, total // 2), f32)
            for axis in range(3):
                spread = block[:, axis : axis + 1] - ordered_rows[axis : axis + 1, wide]
                squared = squared + spread * spread
            spacing = squared * lax.rsqrt(squared)
            turns = spacing * (1.0 / math.pi)
            rest = turns - jnp.round(turns)
            value = polynomial(tuple(scale * t for t in COS_TERMS), rest * rest) / (1.0 + spacing)
            col = ordered_rows[5:6, wide]
            linked = (col >= low) & (col <= high)
            trans[pl.ds(first, 16), wide] = jnp.where(linked, 0.0, value).astype(bf16)
        return carry

    lax.fori_loop(0, total // 16, translation, 0, unroll=4)

    fetch_agg.wait()

    def gather(g, carry):
        span = pl.ds(pl.multiple_of(g * 256, 256), 256)
        pltpu.make_async_copy(in1.at[span], in1.at[span], recv1.at[g]).wait()
        product = dot_nt(in1[span, :], agg_ref[...]).reshape(16, 2, 8, 2 * dir_count)
        real = product[:, 0].reshape(128, 2 * dir_count)
        imag = product[:, 1].reshape(128, 2 * dir_count)
        pat_re = real[:, :dir_count] - imag[:, dir_count:]
        pat_im = real[:, dir_count:] + imag[:, :dir_count]
        own = pl.ds(pl.multiple_of(g * 128, 128), 128)
        cosine = cos_t[own, :]
        sine = sin_t[own, :]
        pattern[own, :dir_count] = (cosine * pat_re + sine * pat_im).astype(bf16)
        pattern[own, dir_count:] = (cosine * pat_im - sine * pat_re).astype(bf16)
        return carry

    early = groups * 1 // 2
    known = total * 1 // 2
    lax.fori_loop(0, early, gather, 0)

    def begin(q, carry):
        own = pl.ds(pl.multiple_of(q * 256, 256), 256)
        partial[own, :] = dot_nn(trans[own, :known], pattern[:known, :])
        return carry

    lax.fori_loop(0, total // 256, begin, 0)
    lax.fori_loop(early, groups, gather, 0)

    fetch_dis.wait()

    def spread(q, carry):
        own = pl.ds(pl.multiple_of(q * 128, 128), 128)
        summed = partial[own, :] + dot_nn(trans[own, known:], pattern[known:, :])
        sum_re = summed[:, :dir_count]
        sum_im = summed[:, dir_count:]
        cosine = cos_t[own, :]
        sine = sin_t[own, :]
        rec_re = (cosine * sum_re - sine * sum_im).astype(bf16)
        rec_im = (cosine * sum_im + sine * sum_re).astype(bf16)
        from_re = dot_nt(rec_re, dis_ref[...])
        from_im = dot_nt(rec_im, dis_ref[...])
        far_re = from_re[:, :nu] - from_im[:, nu:]
        far_im = from_im[:, :nu] + from_re[:, nu:]
        both = jnp.concatenate(
            [far_re.reshape(16, 1, 8, nu), far_im.reshape(16, 1, 8, nu)], axis=1
        ).reshape(256, nu)
        out2[pl.ds(pl.multiple_of(q * 256, 256), 256), :] = both.astype(bf16)

        for half in range(1):
            i = q
            base = me ^ spread_high(flip(i))
            for v in range(16):
                copy = pltpu.make_async_remote_copy(
                    src_ref=out2.at[slot(i * 16 + (my_low ^ v))],
                    dst_ref=in2.at[slot(i * 16 + my_low)],
                    send_sem=send2,
                    recv_sem=recv2.at[i],
                    device_id=place(base ^ spread_low(v)),
                    device_id_type=MESH,
                )
                if half == 0 and v == 0:
                    pl.when(q > 0)(copy.start)
                else:
                    copy.start()
        return carry

    lax.fori_loop(0, groups, spread, 0)
    pltpu.make_async_copy(out2.at[slot(my_low)], in2.at[slot(my_low)], recv2.at[0]).start()

    to_right.wait_recv()
    to_left.wait_recv()
    padded[0, :, :angles] = halo[0, 0]
    padded[0, :, angles:] = halo[0, 1]
    padded[boxes + 1, :, :angles] = halo[1, 0]
    padded[boxes + 1, :, angles:] = halo[1, 1]

    def widen(b, carry):
        padded[b + 1, :, :angles] = cur_ref[b, 0]
        padded[b + 1, :, angles:] = cur_ref[b, 1]
        return carry

    lax.fori_loop(0, boxes, widen, 0)
    fetch_near.wait()

    def near(b, carry):
        box = me * boxes + b
        left = jnp.where(box > 0, mask_smem[0, box], 0).astype(f32)
        right = jnp.where(box < total - 1, mask_smem[1, box], 0).astype(f32)
        sides = []
        for part in range(2):
            sides.append(
                dot_nn(near_v[b, 0, part], padded[b + 1])
                + left * dot_nn(near_v[b, 1, part], padded[b])
                + right * dot_nn(near_v[b, 2, part], padded[b + 2])
            )
        near_sum[b, 0] = sides[0][:, :angles] - sides[1][:, angles:]
        near_sum[b, 1] = sides[0][:, angles:] + sides[1][:, :angles]
        return carry

    lax.fori_loop(0, boxes, near, 0, unroll=2)

    def unpack(g, carry):
        span = pl.ds(pl.multiple_of(g * 256, 256), 256)
        pltpu.make_async_copy(in2.at[span], in2.at[span], recv2.at[g]).wait()
        block = dot_nn(swap, in2[span, :]).astype(bf16).reshape(rows, 16, nu)
        turned[:, slot(my_high ^ flip(g)), :] = block
        return carry

    lax.fori_loop(0, groups, unpack, 0)

    def finish(pair, carry):
        far = dot_nt(eye_unknown, turned[pl.ds(pair * 2, 2)].reshape(2 * angles, nu))
        for k in range(2):
            r = pair * 2 + k
            b = r & (boxes - 1)
            p = r // boxes
            out_ref[b, p] = (far[:, k * angles : (k + 1) * angles] + near_sum[b, p]).astype(bf16)
        return carry

    lax.fori_loop(0, rows // 2, finish, 0, unroll=8)

    sent = pl.ds(0, (n - 1) * 16)
    pltpu.make_async_copy(out1.at[sent], in1.at[sent], send1).wait()
    pltpu.make_async_copy(out2.at[sent], in2.at[sent], send2).wait()
    to_right.wait_send()
    to_left.wait_send()


def local(n, dirs, currents, near_blocks, near_mask, aggregate, disaggregate, centers):
    boxes, _, nu, angles = currents.shape
    dir_count = aggregate.shape[1]
    total = n * boxes
    f32, bf16 = jnp.float32, jnp.bfloat16
    vmem = pl.BlockSpec(memory_space=pltpu.VMEM)
    anywhere = pl.BlockSpec(memory_space=pl.ANY)
    return pl.pallas_call(
        functools.partial(kernel, n, dirs),
        out_shape=pltpu.VMEM(currents.shape, bf16),
        in_specs=[
            anywhere,
            anywhere,
            anywhere,
            anywhere,
            anywhere,
            anywhere,
            anywhere,
        ],
        out_specs=vmem,
        scratch_shapes=[
            pltpu.VMEM(near_mask.shape, jnp.int32),
            pltpu.SMEM(near_mask.shape, jnp.int32),
            pltpu.VMEM(centers.shape, f32),
            pltpu.VMEM((8, dir_count), f32),
            pltpu.VMEM(currents.shape, bf16),
            pltpu.VMEM((2 * dir_count, nu), bf16),
            pltpu.VMEM((2 * nu, dir_count), bf16),
            pltpu.VMEM(near_blocks.shape, bf16),
            pltpu.SemaphoreType.DMA((8,)),
            pltpu.VMEM((2, 2, nu, angles), bf16),
            pltpu.SemaphoreType.DMA((2,)),
            pltpu.SemaphoreType.DMA((2,)),
            pltpu.VMEM((2 * boxes, angles, nu), bf16),
            pltpu.VMEM((n * 16, nu), bf16),
            pltpu.VMEM((n * 16, nu), bf16),
            pltpu.SemaphoreType.DMA,
            pltpu.SemaphoreType.DMA((n // 16,)),
            pltpu.VMEM((total, 8), f32),
            pltpu.VMEM((total, 8), f32),
            pltpu.VMEM((8, total), f32),
            pltpu.VMEM((total, dir_count), f32),
            pltpu.VMEM((total, dir_count), f32),
            pltpu.VMEM((total, total), bf16),
            pltpu.VMEM((total, 2 * dir_count), bf16),
            pltpu.VMEM((n * 16, nu), bf16),
            pltpu.VMEM((n * 16, nu), bf16),
            pltpu.SemaphoreType.DMA,
            pltpu.SemaphoreType.DMA((n // 16,)),
            pltpu.VMEM((boxes + 2, nu, 2 * angles), bf16),
            pltpu.VMEM((boxes, 2, nu, angles), f32),
            pltpu.VMEM((total, 2 * dir_count), f32),
        ],
        compiler_params=pltpu.CompilerParams(
            collective_id=0, has_side_effects=True, vmem_limit_bytes=56 * 1024 * 1024
        ),
    )(
        currents,
        near_blocks,
        near_mask,
        aggregate.reshape(2 * dir_count, nu),
        disaggregate.reshape(2 * nu, dir_count),
        centers,
        jnp.asarray(direction_turns(dir_count)),
    )


def solution(mesh):
    dirs = mesh.shape["dir"]
    return jax.shard_map(
        functools.partial(local, mesh.shape["box"] * dirs, dirs),
        mesh=mesh,
        in_specs=(
            P(("box", "dir"), None, None, None),
            P(("box", "dir"), None, None, None, None),
            P(),
            P(),
            P(),
            P(),
        ),
        out_specs=P(("box", "dir"), None, None, None),
        check_vma=False,
    )
```

```python
import functools
import math

import jax
import jax.numpy as jnp
import numpy as np
from jax import lax
from jax.experimental import pallas as pl
from jax.experimental.pallas import tpu as pltpu
from jax.sharding import PartitionSpec as P

MESH = pl.DeviceIdType.MESH
golden_turn = 2.399963229728653
far_gain = 8.0

COS_TERMS = (
    1.0,
    -19.73920440673828,
    64.93911743164062,
    -85.45014190673828,
    60.16762924194336,
    -25.967599868774414,
    6.528658390045166,
)
SIN_TERMS = (
    6.2831854820251465,
    -41.34170150756836,
    81.60513305664062,
    -76.70301818847656,
    42.02592849731445,
    -14.899847030639648,
    3.2381374835968018,
)


def polynomial(terms, x):
    total = x * terms[-1] + terms[-2]
    for term in terms[-3::-1]:
        total = total * x + term
    return total


def direction_turns(count):
    order = np.arange(count, dtype=np.float32)
    height = np.float32(1.0) - (np.float32(2.0) * order + np.float32(1.0)) / np.float32(count)
    radial = np.sqrt(np.float32(1.0) - height * height)
    azimuth = (order * np.float32(golden_turn)).astype(np.float64)
    rows = [radial * np.cos(azimuth), radial * np.sin(azimuth), height.astype(np.float64)]
    table = np.zeros((8, count), np.float32)
    for row, values in enumerate(rows):
        table[row] = (values / math.pi).astype(np.float32)
    return table


def dot_nt(left, right):
    return lax.dot_general(left, right, (((1,), (1,)), ((), ())), preferred_element_type=jnp.float32)


def dot_nn(left, right):
    return jnp.dot(left, right, preferred_element_type=jnp.float32)


def kernel(
    n,
    dirs,
    cur_hbm,
    near_hbm,
    mask_hbm,
    agg_hbm,
    dis_hbm,
    cen_hbm,
    turn_hbm,
    out_ref,
    mask_ref,
    mask_smem,
    cen_ref,
    turn_ref,
    cur_ref,
    agg_ref,
    dis_ref,
    near_v,
    fetch_sem,
    halo,
    halo_send,
    halo_recv,
    turned,
    out1,
    in1,
    send1,
    recv1,
    columns,
    ordered,
    ordered_rows,
    cos_t,
    sin_t,
    trans,
    pattern,
    out2,
    in2,
    send2,
    recv2,
    padded,
    near_sum,
    partial,
):
    f32, bf16 = jnp.float32, jnp.bfloat16
    boxes, _, nu, angles = cur_ref.shape
    rows = 2 * boxes
    total = n * boxes
    dir_count = agg_ref.shape[0] // 2
    groups = n // 16
    me = lax.axis_index("box") * dirs + lax.axis_index("dir")

    def place(device):
        return (device // dirs, lax.rem(device, dirs))

    fetch_cur = pltpu.make_async_copy(cur_hbm, cur_ref, fetch_sem.at[0])
    fetch_agg = pltpu.make_async_copy(agg_hbm, agg_ref, fetch_sem.at[1])
    fetch_dis = pltpu.make_async_copy(dis_hbm, dis_ref, fetch_sem.at[2])
    fetch_near = pltpu.make_async_copy(near_hbm, near_v, fetch_sem.at[3])
    small = [
        pltpu.make_async_copy(cen_hbm, cen_ref, fetch_sem.at[4]),
        pltpu.make_async_copy(turn_hbm, turn_ref, fetch_sem.at[5]),
        pltpu.make_async_copy(mask_hbm, mask_ref, fetch_sem.at[6]),
        pltpu.make_async_copy(mask_hbm, mask_smem, fetch_sem.at[7]),
    ]
    fetch_cur.start()

    barrier = pltpu.get_barrier_semaphore()

    def greet(device):
        pl.semaphore_signal(barrier, inc=1, device_id=place(device), device_id_type=MESH)

    root = 122
    first = (me // 16) * 16 + 10

    @pl.when(me != root)
    def _():
        greet(root)

    def equal(shape, row_of, col_of):
        row = lax.broadcasted_iota(jnp.int32, shape, 0)
        col = lax.broadcasted_iota(jnp.int32, shape, 1)
        return jnp.where(row_of(row) == col_of(col), 1.0, 0.0).astype(bf16)

    eye_angle = equal((angles, angles), lambda r: r, lambda c: c)
    eye_unknown = equal((nu, nu), lambda r: r, lambda c: c)
    swap = equal((256, 256), lambda r: r, lambda c: (c & 15) * 16 + (c >> 4))

    fetch_cur.wait()
    fetch_agg.start()
    fetch_dis.start()
    for copy in small:
        copy.start()

    def turn(r, carry):
        block = cur_ref[r & (boxes - 1), r // boxes]
        turned[r] = dot_nt(eye_angle, block).astype(bf16)
        return carry

    lax.fori_loop(0, rows, turn, 0, unroll=4)

    def pack(g, carry):
        first = pl.multiple_of(g * 16, 16)
        block = turned[:, pl.ds(first, 16), :].reshape(256, nu)
        out1[pl.ds(pl.multiple_of(g * 256, 256), 256), :] = dot_nn(swap, block).astype(bf16)
        return carry

    lax.fori_loop(0, groups, pack, 0, unroll=4)


    @pl.when(me == root)
    def _():
        pl.semaphore_wait(barrier, n - 1)
        for k in range(n // 16):
            if k * 16 + 10 != root:
                greet(k * 16 + 10)

    @pl.when(me != root)
    def _():
        pl.semaphore_wait(barrier, 1)

    @pl.when(me == first)
    def _():
        for k in range(16):
            if k != 10:
                greet((me // 16) * 16 + k)


    my_high = ((me >> 4) & 4) | ((me >> 2) & 2) | ((me >> 1) & 1)
    my_low = ((me >> 2) & 12) | ((me >> 1) & 2) | (me & 1)

    def flip(i):
        return jnp.where((i & 1) == 0, i >> 1, 7 - (i >> 1))

    def spread_high(high):
        return ((high & 4) << 4) | ((high & 2) << 2) | ((high & 1) << 1)

    def spread_low(low):
        return ((low & 12) << 2) | ((low & 2) << 1) | (low & 1)

    def slot(position):
        return pl.ds(pl.multiple_of(position * 16, 16), 16)

    def send_out1(i, first):
        base = me ^ spread_high(flip(i))
        angle_base = (my_high ^ flip(i)) * 16
        for v in range(first, 16):
            pltpu.make_async_remote_copy(
                src_ref=out1.at[slot(angle_base + (my_low ^ v))],
                dst_ref=in1.at[slot(i * 16 + my_low)],
                send_sem=send1,
                recv_sem=recv1.at[i],
                device_id=place(base ^ spread_low(v)),
                device_id_type=MESH,
            ).start()

    send_out1(0, 1)

    def send_group(i, carry):
        send_out1(i, 0)
        return carry

    lax.fori_loop(1, groups, send_group, 0)
    pltpu.make_async_copy(
        out1.at[slot(my_high * 16 + my_low)], in1.at[slot(my_low)], recv1.at[0]
    ).start()

    to_right = pltpu.make_async_remote_copy(
        src_ref=cur_ref.at[boxes - 1],
        dst_ref=halo.at[0],
        send_sem=halo_send.at[0],
        recv_sem=halo_recv.at[0],
        device_id=place(lax.rem(me + 1, n)),
        device_id_type=MESH,
    )
    to_left = pltpu.make_async_remote_copy(
        src_ref=cur_ref.at[0],
        dst_ref=halo.at[1],
        send_sem=halo_send.at[1],
        recv_sem=halo_recv.at[1],
        device_id=place(lax.rem(me + n - 1, n)),
        device_id_type=MESH,
    )
    fetch_near.start()

    for copy in small:
        copy.wait()

    box_row = lax.broadcasted_iota(jnp.int32, (1, total), 1).astype(f32)
    low_row = box_row - mask_ref[0:1, :].astype(f32)
    high_row = box_row + mask_ref[1:2, :].astype(f32)
    table = jnp.concatenate(
        [cen_ref[...], low_row, high_row, box_row, jnp.zeros((2, total), f32)], axis=0
    )
    columns[...] = jnp.transpose(table)

    def order(i, carry):
        base = spread_high(my_high ^ flip(i))
        for low in range(16):
            source = pl.ds(pl.multiple_of((base | spread_low(low)) * 8, 8), 8)
            ordered[pl.ds(pl.multiple_of((i * 16 + low) * 8, 8), 8), :] = columns[source, :]
        return carry

    lax.fori_loop(0, groups, order, 0)
    ordered_rows[...] = jnp.transpose(ordered[...])

    def phase(step, carry):
        own = pl.ds(pl.multiple_of(step * 16, 16), 16)
        block = ordered[own, :]
        turns = (
            block[:, 0:1] * turn_ref[0:1, :]
            + block[:, 1:2] * turn_ref[1:2, :]
            + block[:, 2:3] * turn_ref[2:3, :]
        )
        rest = turns - jnp.round(turns)
        square = rest * rest
        cos_t[own, :] = polynomial(COS_TERMS, square)
        sin_t[own, :] = rest * polynomial(SIN_TERMS, square)
        return carry

    lax.fori_loop(0, total // 16, phase, 0, unroll=4)
    to_right.start()
    to_left.start()

    scale = far_gain / math.sqrt(total)

    def translation(step, carry):
        first = pl.multiple_of(step * 16, 16)
        block = ordered[pl.ds(first, 16), :]
        low = block[:, 3:4]
        high = block[:, 4:5]
        for part in range(2):
            wide = slice(part * (total // 2), (part + 1) * (total // 2))
            squared = jnp.ones((16, total // 2), f32)
            for axis in range(3):
                spread = block[:, axis : axis + 1] - ordered_rows[axis : axis + 1, wide]
                squared = squared + spread * spread
            spacing = squared * lax.rsqrt(squared)
            turns = spacing * (1.0 / math.pi)
            rest = turns - jnp.round(turns)
            value = polynomial(tuple(scale * t for t in COS_TERMS), rest * rest) / (1.0 + spacing)
            col = ordered_rows[5:6, wide]
            linked = (col >= low) & (col <= high)
            trans[pl.ds(first, 16), wide] = jnp.where(linked, 0.0, value).astype(bf16)
        return carry

    lax.fori_loop(0, total // 16, translation, 0, unroll=4)

    fetch_agg.wait()

    def gather(g, carry):
        span = pl.ds(pl.multiple_of(g * 256, 256), 256)
        pltpu.make_async_copy(in1.at[span], in1.at[span], recv1.at[g]).wait()
        product = dot_nt(in1[span, :], agg_ref[...]).reshape(16, 2, 8, 2 * dir_count)
        real = product[:, 0].reshape(128, 2 * dir_count)
        imag = product[:, 1].reshape(128, 2 * dir_count)
        pat_re = real[:, :dir_count] - imag[:, dir_count:]
        pat_im = real[:, dir_count:] + imag[:, :dir_count]
        own = pl.ds(pl.multiple_of(g * 128, 128), 128)
        cosine = cos_t[own, :]
        sine = sin_t[own, :]
        pattern[own, :dir_count] = (cosine * pat_re + sine * pat_im).astype(bf16)
        pattern[own, dir_count:] = (cosine * pat_im - sine * pat_re).astype(bf16)
        return carry

    early = groups * 1 // 2
    known = total * 1 // 2
    lax.fori_loop(0, early, gather, 0)

    def begin(q, carry):
        own = pl.ds(pl.multiple_of(q * 256, 256), 256)
        partial[own, :] = dot_nn(trans[own, :known], pattern[:known, :])
        return carry

    lax.fori_loop(0, total // 256, begin, 0)
    lax.fori_loop(early, groups, gather, 0)

    fetch_dis.wait()

    def spread(q, carry):
        own = pl.ds(pl.multiple_of(q * 128, 128), 128)
        summed = partial[own, :] + dot_nn(trans[own, known:], pattern[known:, :])
        sum_re = summed[:, :dir_count]
        sum_im = summed[:, dir_count:]
        cosine = cos_t[own, :]
        sine = sin_t[own, :]
        rec_re = (cosine * sum_re - sine * sum_im).astype(bf16)
        rec_im = (cosine * sum_im + sine * sum_re).astype(bf16)
        from_re = dot_nt(rec_re, dis_ref[...])
        from_im = dot_nt(rec_im, dis_ref[...])
        far_re = from_re[:, :nu] - from_im[:, nu:]
        far_im = from_im[:, :nu] + from_re[:, nu:]
        both = jnp.concatenate(
            [far_re.reshape(16, 1, 8, nu), far_im.reshape(16, 1, 8, nu)], axis=1
        ).reshape(256, nu)
        out2[pl.ds(pl.multiple_of(q * 256, 256), 256), :] = both.astype(bf16)

        for half in range(1):
            i = q
            base = me ^ spread_high(flip(i))
            for v in range(16):
                copy = pltpu.make_async_remote_copy(
                    src_ref=out2.at[slot(i * 16 + (my_low ^ v))],
                    dst_ref=in2.at[slot(i * 16 + my_low)],
                    send_sem=send2,
                    recv_sem=recv2.at[i],
                    device_id=place(base ^ spread_low(v)),
                    device_id_type=MESH,
                )
                if half == 0 and v == 0:
                    pl.when(q > 0)(copy.start)
                else:
                    copy.start()
        return carry

    lax.fori_loop(0, groups, spread, 0)
    pltpu.make_async_copy(out2.at[slot(my_low)], in2.at[slot(my_low)], recv2.at[0]).start()

    to_right.wait_recv()
    to_left.wait_recv()
    padded[0, :, :angles] = halo[0, 0]
    padded[0, :, angles:] = halo[0, 1]
    padded[boxes + 1, :, :angles] = halo[1, 0]
    padded[boxes + 1, :, angles:] = halo[1, 1]

    def widen(b, carry):
        padded[b + 1, :, :angles] = cur_ref[b, 0]
        padded[b + 1, :, angles:] = cur_ref[b, 1]
        return carry

    lax.fori_loop(0, boxes, widen, 0)
    fetch_near.wait()

    def near(b, carry):
        box = me * boxes + b
        left = jnp.where(box > 0, mask_smem[0, box], 0).astype(f32)
        right = jnp.where(box < total - 1, mask_smem[1, box], 0).astype(f32)
        sides = []
        for part in range(2):
            sides.append(
                dot_nn(near_v[b, 0, part], padded[b + 1])
                + left * dot_nn(near_v[b, 1, part], padded[b])
                + right * dot_nn(near_v[b, 2, part], padded[b + 2])
            )
        near_sum[b, 0] = sides[0][:, :angles] - sides[1][:, angles:]
        near_sum[b, 1] = sides[0][:, angles:] + sides[1][:, :angles]
        return carry

    lax.fori_loop(0, boxes, near, 0, unroll=2)

    def unpack(g, carry):
        span = pl.ds(pl.multiple_of(g * 256, 256), 256)
        pltpu.make_async_copy(in2.at[span], in2.at[span], recv2.at[g]).wait()
        block = dot_nn(swap, in2[span, :]).astype(bf16).reshape(rows, 16, nu)
        turned[:, slot(my_high ^ flip(g)), :] = block
        return carry

    lax.fori_loop(0, groups, unpack, 0)

    def finish(pair, carry):
        far = dot_nt(eye_unknown, turned[pl.ds(pair * 2, 2)].reshape(2 * angles, nu))
        for k in range(2):
            r = pair * 2 + k
            b = r & (boxes - 1)
            p = r // boxes
            out_ref[b, p] = (far[:, k * angles : (k + 1) * angles] + near_sum[b, p]).astype(bf16)
        return carry

    lax.fori_loop(0, rows // 2, finish, 0, unroll=8)

    sent = pl.ds(0, (n - 1) * 16)
    pltpu.make_async_copy(out1.at[sent], in1.at[sent], send1).wait()
    pltpu.make_async_copy(out2.at[sent], in2.at[sent], send2).wait()
    to_right.wait_send()
    to_left.wait_send()


def local(n, dirs, currents, near_blocks, near_mask, aggregate, disaggregate, centers):
    boxes, _, nu, angles = currents.shape
    dir_count = aggregate.shape[1]
    total = n * boxes
    f32, bf16 = jnp.float32, jnp.bfloat16
    vmem = pl.BlockSpec(memory_space=pltpu.VMEM)
    anywhere = pl.BlockSpec(memory_space=pl.ANY)
    return pl.pallas_call(
        functools.partial(kernel, n, dirs),
        out_shape=pltpu.VMEM(currents.shape, bf16),
        in_specs=[
            anywhere,
            anywhere,
            anywhere,
            anywhere,
            anywhere,
            anywhere,
            anywhere,
        ],
        out_specs=vmem,
        scratch_shapes=[
            pltpu.VMEM(near_mask.shape, jnp.int32),
            pltpu.SMEM(near_mask.shape, jnp.int32),
            pltpu.VMEM(centers.shape, f32),
            pltpu.VMEM((8, dir_count), f32),
            pltpu.VMEM(currents.shape, bf16),
            pltpu.VMEM((2 * dir_count, nu), bf16),
            pltpu.VMEM((2 * nu, dir_count), bf16),
            pltpu.VMEM(near_blocks.shape, bf16),
            pltpu.SemaphoreType.DMA((8,)),
            pltpu.VMEM((2, 2, nu, angles), bf16),
            pltpu.SemaphoreType.DMA((2,)),
            pltpu.SemaphoreType.DMA((2,)),
            pltpu.VMEM((2 * boxes, angles, nu), bf16),
            pltpu.VMEM((n * 16, nu), bf16),
            pltpu.VMEM((n * 16, nu), bf16),
            pltpu.SemaphoreType.DMA,
            pltpu.SemaphoreType.DMA((n // 16,)),
            pltpu.VMEM((total, 8), f32),
            pltpu.VMEM((total, 8), f32),
            pltpu.VMEM((8, total), f32),
            pltpu.VMEM((total, dir_count), f32),
            pltpu.VMEM((total, dir_count), f32),
            pltpu.VMEM((total, total), bf16),
            pltpu.VMEM((total, 2 * dir_count), bf16),
            pltpu.VMEM((n * 16, nu), bf16),
            pltpu.VMEM((n * 16, nu), bf16),
            pltpu.SemaphoreType.DMA,
            pltpu.SemaphoreType.DMA((n // 16,)),
            pltpu.VMEM((boxes + 2, nu, 2 * angles), bf16),
            pltpu.VMEM((boxes, 2, nu, angles), f32),
            pltpu.VMEM((total, 2 * dir_count), f32),
        ],
        compiler_params=pltpu.CompilerParams(
            collective_id=0, has_side_effects=True, vmem_limit_bytes=56 * 1024 * 1024
        ),
    )(
        currents,
        near_blocks,
        near_mask,
        aggregate.reshape(2 * dir_count, nu),
        disaggregate.reshape(2 * nu, dir_count),
        centers,
        jnp.asarray(direction_turns(dir_count)),
    )


def solution(mesh):
    dirs = mesh.shape["dir"]
    return jax.shard_map(
        functools.partial(local, mesh.shape["box"] * dirs, dirs),
        mesh=mesh,
        in_specs=(
            P(("box", "dir"), None, None, None),
            P(("box", "dir"), None, None, None, None),
            P(),
            P(),
            P(),
            P(),
        ),
        out_specs=P(("box", "dir"), None, None, None),
        check_vma=False,
    )
```
